256 devices in a mesh: view: 2 (over x_hi), frame: 32 (over z, x_lo, core), dp: 4 (over y).
Axes of the slice: x: 4 (x_hi: 2, x_lo: 2; x = x_hi * 2 + x_lo), y: 4, z: 8, core: 2. Of those that a mesh axis runs over, the one named last changes fastest.
Arguments:
- level_in: bfloat16 [8, 32, 128, 640], P('view', 'frame', 'dp'), may hold values from -6 to 6
- out_grad: bfloat16 [8, 32, 128, 640], P('view', 'frame', 'dp'), may hold values from -6 to 6
- view_qkv: bfloat16 [640, 1920], replicated, may hold values from -0.25 to 0.25
- view_out: bfloat16 [640, 640], replicated, may hold values from -0.25 to 0.25
- time_qkv: bfloat16 [640, 1920], replicated, may hold values from -0.25 to 0.25
- time_out: bfloat16 [640, 640], replicated, may hold values from -0.25 to 0.25
Outputs:
- level_out: bfloat16 [8, 32, 128, 640], P('view', 'frame', 'dp')
- level_in_grad: bfloat16 [8, 32, 128, 640], P('view', 'frame', 'dp')
- view_qkv_grad: bfloat16 [640, 1920], P(('frame', 'dp'))
- view_out_grad: bfloat16 [640, 640], P(('frame', 'dp'))
- time_qkv_grad: bfloat16 [640, 1920], P(('frame', 'dp'))
- time_out_grad: bfloat16 [640, 640], P(('frame', 'dp'))
- norm_back_sums: float32 [2, 2, 8, 32, 32], P(None, None, 'view', 'frame')
The draws below stay inside these ranges and needn't reach their ends.
All inputs are finite; a program needn't handle non-finite values.
Results may differ from the reference program's by a relative error of at most 0.025.
Values may be sent and summed in bfloat16 or wider, within the bound.
No kernel may reach another device: no remote copies, remote signals or barrier semaphores. Data moves between devices by JAX's collectives and lax.ppermute only.
A program may use at most 128 MiB of HBM per device.

```python
import jax
import jax.numpy as jnp
from jax import lax

D = 640
HEADS = 10
HD = 64
GROUPS = 32
VIEWS = 8
FRAMES = 32
PIXELS = 128


def steps_of(rng, shape, pieces, low, largest):
    level = 1.0
    for position, blocks in pieces:
        steps = jax.random.uniform(jax.random.fold_in(jax.random.fold_in(rng, 6), position), (blocks,), jnp.float32, low / len(pieces), largest / len(pieces))
        level = level * jnp.repeat(jnp.exp(steps), shape[position] // blocks).reshape((-1,) + (1,) * (len(shape) - 1 - position))
    return level


def noise(key, dims, scale, limit, pieces=(), dtype=jnp.bfloat16):
    loudness = steps_of(key, dims, pieces, -0.22, 0.18) if pieces else 1.0
    drawn = jax.random.normal(key, dims, jnp.float32) * scale * loudness
    return jnp.minimum(jnp.maximum(drawn, -limit), limit).astype(dtype)


def setup_inputs(seed: int = 0) -> dict:
    streams_of = jax.random.split(jax.random.key(seed), 7)
    return {
        "level_in": noise(streams_of[0], (VIEWS, FRAMES, PIXELS, D), 1.0, 6.0, ((0, 2), (1, 32), (2, 4))),
        "out_grad": noise(streams_of[1], (VIEWS, FRAMES, PIXELS, D), 1.0, 6.0, ((0, 2), (1, 32), (2, 4))),
        "view_qkv": noise(streams_of[2], (D, 3 * D), D ** -0.5, 0.25),
        "view_out": noise(streams_of[3], (D, D), D ** -0.5, 0.25),
        "time_qkv": noise(streams_of[4], (D, 3 * D), D ** -0.5, 0.25),
        "time_out": noise(streams_of[5], (D, D), D ** -0.5, 0.25),
    }


EPS = 1e-05

def to_sequence(tensor, attend_dim):
    return jnp.moveaxis(tensor, attend_dim, 2).reshape(-1, tensor.shape[attend_dim], tensor.shape[-1])

def from_sequence(flattened, attend_dim, target_shape):
    remaining = [target_shape[member] for member in range(3) if member != attend_dim]
    tensor = flattened.reshape(remaining[0], remaining[1], target_shape[attend_dim], flattened.shape[-1])
    return jnp.moveaxis(tensor, 2, attend_dim)

def mixing(tensor, matrix):
    flattened = tensor.reshape(-1, tensor.shape[-1])
    product = jnp.dot(flattened, matrix, preferred_element_type=jnp.float32)
    return product.reshape(tensor.shape[:-1] + (matrix.shape[1],))

def project(tensor, matrix):
    return mixing(tensor, matrix).astype(jnp.bfloat16)

def project_back(tensor, matrix):
    flattened = tensor.reshape(-1, tensor.shape[-1])
    product = lax.dot_general(flattened, matrix, (((1,), (1,)), ((), ())), preferred_element_type=jnp.float32)
    return product.astype(jnp.bfloat16).reshape(tensor.shape[:-1] + (matrix.shape[0],))

def weight_grad(left_side, right_side):
    return lax.dot_general(left_side.reshape(-1, left_side.shape[-1]), right_side.reshape(-1, right_side.shape[-1]), (((0,), (0,)), ((), ())), preferred_element_type=jnp.float32)

def split_heads(tensor):
    return tensor.reshape(tensor.shape[0], tensor.shape[1], HEADS, -1).astype(jnp.float32)

def attend(queries, key_rows, value_rows):
    scaling = HD ** (-0.5)
    scores = jnp.einsum('bqhe,bkhe->bhqk', split_heads(queries), split_heads(key_rows), precision=lax.Precision.HIGHEST) * scaling
    softmax_out = jax.nn.softmax(scores, axis=-1)
    rounded = softmax_out.astype(jnp.bfloat16).astype(jnp.float32)
    combined = jnp.einsum('bhqk,bkhe->bqhe', rounded, split_heads(value_rows), precision=lax.Precision.HIGHEST)
    return (combined.astype(jnp.bfloat16).reshape(queries.shape), softmax_out)

def attend_back(upstream, queries, key_rows, value_rows, softmax_out):
    scaling = HD ** (-0.5)
    upstream_heads = split_heads(upstream)
    rounded = softmax_out.astype(jnp.bfloat16).astype(jnp.float32)
    dvalue = jnp.einsum('bhqk,bqhe->bkhe', rounded, upstream_heads, precision=lax.Precision.HIGHEST)
    dprob = jnp.einsum('bqhe,bkhe->bhqk', upstream_heads, split_heads(value_rows), precision=lax.Precision.HIGHEST)
    dscore = softmax_out * (dprob - lax.optimization_barrier(jnp.sum(dprob * softmax_out, axis=-1, keepdims=True)))
    dscore_b = (dscore * scaling).astype(jnp.bfloat16).astype(jnp.float32)
    dquery = jnp.einsum('bhqk,bkhe->bqhe', dscore_b, split_heads(key_rows), precision=lax.Precision.HIGHEST)
    dkey = jnp.einsum('bhqk,bqhe->bkhe', dscore_b, split_heads(queries), precision=lax.Precision.HIGHEST)
    return (dquery.reshape(queries.shape), dkey.reshape(key_rows.shape), dvalue.reshape(value_rows.shape))

def norm_forward(tensor):
    shaped = tensor.reshape(tensor.shape[:3] + (GROUPS, -1))
    average = lax.optimization_barrier(jnp.mean(shaped, axis=(2, 4), keepdims=True))
    centred = shaped - average
    variance = lax.optimization_barrier(jnp.mean(centred * centred, axis=(2, 4), keepdims=True))
    inverse = lax.rsqrt(variance + EPS)
    return ((centred * inverse).reshape(tensor.shape), inverse)

def norm_backward(upstream, normed, inverse):
    shaped = upstream.reshape(upstream.shape[:3] + (GROUPS, -1))
    normed_shaped = normed.reshape(shaped.shape)
    count = shaped.shape[2] * shaped.shape[4]
    first_sum = lax.optimization_barrier(jnp.sum(shaped, axis=(2, 4), keepdims=True))
    second_sum = lax.optimization_barrier(jnp.sum(shaped * normed_shaped, axis=(2, 4), keepdims=True))
    result = inverse * (shaped - first_sum / count - normed_shaped * (second_sum / count))
    sums = jnp.stack([first_sum.reshape(shaped.shape[:2] + (GROUPS,)), second_sum.reshape(shaped.shape[:2] + (GROUPS,))])
    return (result.reshape(upstream.shape), sums)

def attention_pieces(packed, attend_dim, width):
    return (to_sequence(packed[..., :width], attend_dim), to_sequence(packed[..., width:2 * width], attend_dim), to_sequence(packed[..., 2 * width:], attend_dim))

def reference(level_in, out_grad, view_qkv, view_out, time_qkv, time_out):
    width = level_in.shape[-1]
    source = level_in.astype(jnp.float32)
    normed_one, inverse_one = norm_forward(source)
    hidden_one = normed_one.astype(jnp.bfloat16)
    packed_one = project(hidden_one, view_qkv)
    query_one, key_one, value_one = attention_pieces(packed_one, 0, width)
    attn_one, soft_one = attend(query_one, key_one, value_one)
    mixed_one = from_sequence(attn_one, 0, level_in.shape)
    stream = source + mixing(mixed_one, view_out)
    normed_two, inverse_two = norm_forward(stream)
    hidden_two = normed_two.astype(jnp.bfloat16)
    packed_two = project(hidden_two, time_qkv)
    query_two, key_two, value_two = attention_pieces(packed_two, 1, width)
    attn_two, soft_two = attend(query_two, key_two, value_two)
    mixed_two = from_sequence(attn_two, 1, level_in.shape)
    temporal = project(mixed_two, time_out)
    level_out = (stream + temporal.astype(jnp.float32)).astype(jnp.bfloat16)
    grad_mixed_two = project_back(out_grad, time_out)
    time_out_total = weight_grad(mixed_two, out_grad)
    dquery_two, dkey_two, dvalue_two = attend_back(to_sequence(grad_mixed_two, 1), query_two, key_two, value_two, soft_two)
    packed_grad_two = jnp.concatenate([from_sequence(member, 1, level_in.shape) for member in (dquery_two, dkey_two, dvalue_two)], axis=-1).astype(jnp.bfloat16)
    time_qkv_total = weight_grad(hidden_two, packed_grad_two)
    grad_hidden_two = project_back(packed_grad_two, time_qkv)
    back_two, sums_two = norm_backward(grad_hidden_two.astype(jnp.float32), normed_two, inverse_two)
    grad_stream = out_grad.astype(jnp.float32) + back_two
    grad_stream_b = grad_stream.astype(jnp.bfloat16)
    grad_mixed_one = project_back(grad_stream_b, view_out)
    view_out_total = weight_grad(mixed_one, grad_stream_b)
    dquery_one, dkey_one, dvalue_one = attend_back(to_sequence(grad_mixed_one, 0), query_one, key_one, value_one, soft_one)
    packed_grad_one = jnp.concatenate([from_sequence(member, 0, level_in.shape) for member in (dquery_one, dkey_one, dvalue_one)], axis=-1).astype(jnp.bfloat16)
    view_qkv_total = weight_grad(hidden_one, packed_grad_one)
    grad_hidden_one = project_back(packed_grad_one, view_qkv)
    back_one, sums_one = norm_backward(grad_hidden_one.astype(jnp.float32), normed_one, inverse_one)
    level_in_grad = (grad_stream + back_one).astype(jnp.bfloat16)
    norm_back_sums = jnp.stack([sums_one, sums_two])
    return (level_out, level_in_grad, view_qkv_total.astype(jnp.bfloat16), view_out_total.astype(jnp.bfloat16), time_qkv_total.astype(jnp.bfloat16), time_out_total.astype(jnp.bfloat16), norm_back_sums)
```

```python
import functools

import jax
import jax.numpy as jnp
from jax import lax
from jax.experimental import pallas as pl
from jax.experimental.pallas import tpu as pltpu
from jax.sharding import Mesh, PartitionSpec as P

HEADS = 10
HD = 64
GROUPS = 32
EPS = 1e-05
D = 640
CH = D // GROUPS
VIEWS = 8
PX = 16
T = VIEWS * PX
HALF = T // 2
SCALE = HD ** (-0.5)
F32 = jnp.float32
BF16 = jnp.bfloat16


def group_matrix():
    row = lax.broadcasted_iota(jnp.int32, (D, 128), 0)
    low = lax.broadcasted_iota(jnp.int32, (D, 128), 1) * CH
    return ((row >= low) & (row < low + CH)).astype(F32)


def to_groups(rows, member):
    return jnp.dot(rows, member, precision=lax.Precision.HIGHEST, preferred_element_type=F32)


def to_channels(groups, member):
    return lax.dot_general(
        groups, member, (((1,), (1,)), ((), ())), precision=lax.Precision.HIGHEST, preferred_element_type=F32
    )


def view_sum(tokens):
    return jnp.sum(tokens.reshape(tokens.shape[0] // PX, PX, D), axis=1)


def per_token(rows):
    return jnp.broadcast_to(rows[:, None, :], (rows.shape[0], PX, D)).reshape(rows.shape[0] * PX, D)


def partial_stats(tokens, member):
    mean = to_groups(view_sum(tokens), member) * (1.0 / (PX * CH))
    centred = tokens - per_token(to_channels(mean, member))
    return mean, to_groups(view_sum(centred * centred), member)


def merge_stats(means, spreads, entries):
    count = len(means)
    mean = sum(means) * (1.0 / count)
    spread = sum(spreads)
    for other in means:
        gap = other - mean
        spread = spread + gap * gap * float(PX * CH)
    return mean, lax.rsqrt(spread * (1.0 / entries) + EPS)


def spread_out(ref, top, bottom):
    both = jnp.concatenate([top, bottom], axis=0)
    ref[...] = jnp.broadcast_to(both[None], ref.shape)


def mm(left, right):
    return jnp.dot(left, right, preferred_element_type=F32)


def mm_t(left, right):
    return lax.dot_general(left, right, (((1,), (1,)), ((), ())), preferred_element_type=F32)


def t_mm(left, right):
    return lax.dot_general(left, right, (((0,), (0,)), ((), ())), preferred_element_type=F32)


def lane_low(rows):
    return lax.broadcasted_iota(jnp.int32, (rows, 128), 1) < HD


def both_heads(pair):
    low = lane_low(pair.shape[0])
    zero = jnp.zeros_like(pair)
    return jnp.concatenate([jnp.where(low, pair, zero), jnp.where(low, zero, pair)], axis=0)


def join_heads(stacked):
    return jnp.where(lane_low(T), stacked[:T], stacked[T:])


def same_sequence(period):
    row = lax.broadcasted_iota(jnp.int32, (2 * T, T), 0)
    col = lax.broadcasted_iota(jnp.int32, (2 * T, T), 1)
    return ((row ^ col) & (period - 1)) == 0


def softmax_pair(stacked_q, keys, allowed):
    scores = jnp.where(allowed, mm_t(stacked_q, keys) * SCALE, -1e30)
    top = jnp.max(scores, axis=-1, keepdims=True)
    weights = jnp.exp(scores - top)
    return weights / jnp.sum(weights, axis=-1, keepdims=True)


def pair_of(index):
    return slice(index * 128, (index + 1) * 128)


def attend(packed, allowed):
    outs = []
    for pair in range(HEADS // 2):
        q = both_heads(packed[:, pair_of(pair)])
        k = packed[:, pair_of(pair + 5)]
        v = packed[:, pair_of(pair + 10)]
        prob = softmax_pair(q, k, allowed).astype(BF16)
        outs.append(join_heads(mm(prob, v)).astype(BF16))
    return jnp.concatenate(outs, axis=1)


def attend_back(grad, packed, allowed):
    dqs, dks, dvs = [], [], []
    for pair in range(HEADS // 2):
        q = both_heads(packed[:, pair_of(pair)])
        k = packed[:, pair_of(pair + 5)]
        v = packed[:, pair_of(pair + 10)]
        g = both_heads(grad[:, pair_of(pair)])
        prob = softmax_pair(q, k, allowed)
        dvs.append(t_mm(prob.astype(BF16), g).astype(BF16))
        dprob = mm_t(g, v)
        dscore = prob * (dprob - jnp.sum(dprob * prob, axis=-1, keepdims=True))
        dscore = (dscore * SCALE).astype(BF16)
        dqs.append(join_heads(mm(dscore, k)).astype(BF16))
        dks.append(t_mm(dscore, q).astype(BF16))
    return jnp.concatenate(dqs + dks + dvs, axis=1)


def k_split(place, x_ref, og_ref, xkeep_ref, ogkeep_ref, send_ref, stats_ref):
    first = place[0] == 0
    member = group_matrix()

    def halves(ref):
        low = ref[:, 0:PX, :].reshape(HALF, D)
        high = ref[:, PX : 2 * PX, :].reshape(HALF, D)
        return jnp.where(first, low, high), jnp.where(first, high, low)

    xkeep, xsend = halves(x_ref)
    ogkeep, ogsend = halves(og_ref)
    xkeep_ref[...] = xkeep
    ogkeep_ref[...] = ogkeep
    send_ref[:, :D] = xsend
    send_ref[:, D:] = ogsend
    tokens = jnp.concatenate([xkeep, xsend], axis=0).astype(F32)
    spread_out(stats_ref, *partial_stats(tokens, member))


def k_view(entries, place, xkeep_ref, ogkeep_ref, recv_ref, g_ref, wqkv_ref, wout_ref,
           stream_ref, packed_ref, mixed_ref, normed_ref, og_ref, own_ref, stats_ref):
    first = place[0] == 0
    member = group_matrix()
    sources = g_ref.shape[0]
    half = VIEWS // 2

    def side(low):
        chosen = range(low, low + sources // 2)
        means = [g_ref[s, a * half : (a + 1) * half, :] for s in chosen for a in range(2)]
        spreads = [g_ref[s, VIEWS + a * half : VIEWS + (a + 1) * half, :] for s in chosen for a in range(2)]
        return merge_stats(means, spreads, entries)

    low, high = side(0), side(sources // 2)
    mean = jnp.concatenate([low[0], high[0]], axis=0)
    inverse = jnp.concatenate([low[1], high[1]], axis=0)
    own_ref[0:VIEWS, :] = mean
    own_ref[VIEWS:, :] = inverse

    def ordered(mine, theirs):
        return jnp.concatenate([jnp.where(first, mine, theirs), jnp.where(first, theirs, mine)], axis=0)

    og_ref[...] = ordered(ogkeep_ref[...], recv_ref[:, D:])
    x = ordered(xkeep_ref[...], recv_ref[:, :D]).astype(F32)
    normed = (x - per_token(to_channels(mean, member))) * per_token(to_channels(inverse, member))
    normed_ref[...] = normed
    packed = mm(normed.astype(BF16), wqkv_ref[...]).astype(BF16)
    packed_ref[...] = packed
    mixed = attend(packed, same_sequence(PX))
    mixed_ref[...] = mixed
    stream = x + mm(mixed, wout_ref[...])
    stream_ref[...] = stream
    spread_out(stats_ref, *partial_stats(stream, member))


def k_norm_two(entries, stream_ref, og_ref, g_ref, send_ref, normed_ref, inverse_ref):
    member = group_matrix()
    sources = range(g_ref.shape[0])
    mean, inverse = merge_stats(
        [g_ref[s, 0:VIEWS, :] for s in sources], [g_ref[s, VIEWS:, :] for s in sources], entries
    )
    inverse_ref[...] = inverse
    normed = (stream_ref[...] - per_token(to_channels(mean, member))) * per_token(to_channels(inverse, member))
    normed_ref[...] = normed
    shape = send_ref.shape[:2] + (D,)
    send_ref[:, :, :D] = normed.astype(BF16).reshape(shape)
    send_ref[:, :, D:] = og_ref[...].reshape(shape)


def weight_sides(core, hidden, mixed, packed_grad, grad, keep_ref, give_ref):
    first = core == 0
    quarter = packed_grad[:, :D], packed_grad[:, D : 2 * D], packed_grad[:, 2 * D :], grad
    keep_ref[:, :D] = hidden
    give_ref[:, :D] = hidden
    keep_ref[:, D : 2 * D] = jnp.where(first, hidden, mixed)
    give_ref[:, D : 2 * D] = jnp.where(first, mixed, hidden)
    for slot in range(2):
        cols = slice((2 + slot) * D, (3 + slot) * D)
        keep_ref[:, cols] = jnp.where(first, quarter[slot], quarter[2 + slot])
        give_ref[:, cols] = jnp.where(first, quarter[2 + slot], quarter[slot])


def k_time(place, recv_ref, wqkv_ref, wout_ref, back_ref, keep_ref, give_ref):
    hidden = recv_ref[:, :, :D].reshape(T, D)
    grad = recv_ref[:, :, D:].reshape(T, D)
    allowed = same_sequence(recv_ref.shape[1])
    packed = mm(hidden, wqkv_ref[...]).astype(BF16)
    mixed = attend(packed, allowed)
    shape = back_ref.shape[:2] + (D,)
    back_ref[:, :, :D] = mm(mixed, wout_ref[...]).astype(BF16).reshape(shape)
    packed_grad = attend_back(mm_t(grad, wout_ref[...]).astype(BF16), packed, allowed)
    back_ref[:, :, D:] = mm_t(packed_grad, wqkv_ref[...]).astype(BF16).reshape(shape)
    weight_sides(place[1], hidden, mixed, packed_grad, grad, keep_ref, give_ref)


def k_level_out(place, back_ref, stream_ref, normed_ref, keep_ref, send_ref, ghid_ref, stats_ref):
    first = place[0] == 0
    member = group_matrix()
    temporal = back_ref[:, :, :D].reshape(T, D)
    ghid = back_ref[:, :, D:].reshape(T, D)
    ghid_ref[...] = ghid
    out = (stream_ref[...] + temporal.astype(F32)).astype(BF16)
    keep_ref[...] = jnp.where(first, out[:HALF], out[HALF:])
    send_ref[...] = jnp.where(first, out[HALF:], out[:HALF])
    grad = ghid.astype(F32)
    spread_out(
        stats_ref,
        to_groups(view_sum(grad), member),
        to_groups(view_sum(grad * normed_ref[...]), member),
    )


def k_view_back(entries, place, ghid_ref, ntwo_ref, itwo_ref, g_ref, og_ref, packed_ref, mixed_ref,
                none_ref, own_ref, wqkv_ref, wout_ref,
                ukeep_ref, usend_ref, keep_ref, give_ref, sums_ref, stats_ref):
    first = place[0] == 0
    member = group_matrix()
    sums = g_ref[0]
    for s in range(1, g_ref.shape[0]):
        sums = sums + g_ref[s]
    sums_ref[...] = sums
    m1 = per_token(to_channels(sums[:VIEWS] * (1.0 / entries), member))
    m2 = per_token(to_channels(sums[VIEWS:] * (1.0 / entries), member))
    inverse = per_token(to_channels(itwo_ref[...], member))
    grad_stream = og_ref[...].astype(F32) + inverse * (ghid_ref[...].astype(F32) - m1 - ntwo_ref[...] * m2)
    grad_b = grad_stream.astype(BF16)
    packed = packed_ref[...]
    packed_grad = attend_back(mm_t(grad_b, wout_ref[...]).astype(BF16), packed, same_sequence(PX))
    normed = none_ref[...]
    weight_sides(place[1], normed.astype(BF16), mixed_ref[...], packed_grad, grad_b, keep_ref, give_ref)
    grad = mm_t(packed_grad, wqkv_ref[...]).astype(BF16).astype(F32)
    spread_out(stats_ref, to_groups(view_sum(grad), member), to_groups(view_sum(grad * normed), member))
    partly = grad_stream + per_token(to_channels(own_ref[VIEWS:, :], member)) * grad
    ukeep_ref[...] = jnp.where(first, partly[:HALF], partly[HALF:])
    usend_ref[...] = jnp.where(first, partly[HALF:], partly[:HALF]).astype(BF16)


def k_finish(entries, place, g_ref, sumstwo_ref, own_ref, xkeep_ref, send_ref, ukeep_ref, urecv_ref,
             okeep_ref, orecv_ref, out_ref, grad_ref, sums_ref):
    first = place[0] == 0
    member = group_matrix()
    half = VIEWS // 2
    sums = g_ref[0]
    for s in range(1, g_ref.shape[0]):
        sums = sums + g_ref[s]

    def mine(rows):
        return jnp.where(first, rows[:half], rows[half:])

    s1, s2 = mine(sums[:VIEWS]), mine(sums[VIEWS:])
    sums_ref[0] = s1
    sums_ref[1] = s2
    sums_ref[2] = mine(sumstwo_ref[0:VIEWS, :])
    sums_ref[3] = mine(sumstwo_ref[VIEWS:, :])
    inverse = mine(own_ref[VIEWS:, :])
    mean_c = per_token(to_channels(mine(own_ref[0:VIEWS, :]), member))
    inverse_c = per_token(to_channels(inverse, member))
    a = per_token(to_channels(inverse * s1 * (1.0 / entries), member))
    b = per_token(to_channels(inverse * s2 * (1.0 / entries), member))

    def finished(part, x):
        normed = (x.astype(F32) - mean_c) * inverse_c
        return (part.astype(F32) - a - normed * b).astype(BF16)

    keep = finished(ukeep_ref[...], xkeep_ref[...])
    other = finished(urecv_ref[...], send_ref[:, :D])
    shape = (half, PX, D)
    grad_ref[:, 0:PX, :] = jnp.where(first, keep, other).reshape(shape)
    grad_ref[:, PX:, :] = jnp.where(first, other, keep).reshape(shape)
    okeep, orecv = okeep_ref[...], orecv_ref[...]
    out_ref[:, 0:PX, :] = jnp.where(first, okeep, orecv).reshape(shape)
    out_ref[:, PX:, :] = jnp.where(first, orecv, okeep).reshape(shape)


def k_weights(order_ref, keep_ref, recv_ref, out_ref):
    for unit in range(2):
        left = jnp.concatenate([keep_ref[:, unit * D : (unit + 1) * D], recv_ref[:, unit * D : (unit + 1) * D]], axis=0)
        cols = slice((2 + unit) * D, (3 + unit) * D)
        right = jnp.concatenate([keep_ref[:, cols], recv_ref[:, cols]], axis=0)
        left = mm(left, order_ref[...]).astype(BF16)
        out_ref[:, unit * D : (unit + 1) * D] = t_mm(left, right).astype(BF16)


def k_sum(parts_ref, out_ref):
    total = parts_ref[0].astype(F32)
    for s in range(1, parts_ref.shape[0]):
        total = total + parts_ref[s].astype(F32)
    total = total.astype(BF16)
    if len(out_ref.shape) == 2:
        out_ref[...] = total
    else:
        rows = out_ref.shape[1]
        for s in range(out_ref.shape[0]):
            out_ref[s] = total[s * rows : (s + 1) * rows]


def call(kernel, outs, *args, place=None):
    vmem = pl.BlockSpec(memory_space=pltpu.VMEM)
    specs = [vmem] * len(args)
    if place is not None:
        specs = [pl.BlockSpec(memory_space=pltpu.SMEM)] + specs
        args = (place,) + args
    return pl.pallas_call(
        kernel,
        out_shape=[jax.ShapeDtypeStruct(shape, dtype) for shape, dtype in outs],
        in_specs=specs,
        out_specs=[vmem] * len(outs),
        compiler_params=pltpu.CompilerParams(vmem_limit_bytes=40 * 1024 * 1024),
    )(*args)


def row_order(z, xl, core, dp):
    rows = D // (z * xl * core * dp)
    place = jnp.arange(D).reshape(z, xl, core, dp, rows).transpose(3, 0, 1, 2, 4).reshape(-1)
    return (jnp.arange(D)[:, None] == place[None, :]).astype(BF16)


def body(sizes, level_in, out_grad, view_qkv, view_out, time_qkv, time_out):
    z, xl, core, dp = sizes
    frames = z * xl * core
    entries = float(dp * 2 * PX * CH)
    frame_axes = ("z", "xl", "core")
    mates = ("view", "dp")
    group = 2 * dp
    place = jnp.stack([lax.axis_index("view"), lax.axis_index("core")]).astype(jnp.int32)
    order = row_order(z, xl, core, dp)
    stats = ((group, 2 * VIEWS, 128), F32)
    tok32, tok16 = ((T, D), F32), ((T, D), BF16)
    half32, half16 = ((HALF, D), F32), ((HALF, D), BF16)
    wide = ((T, 4 * D), BF16)
    moved = ((frames, T // frames, 2 * D), BF16)

    def share(field):
        return lax.all_to_all(field, mates, 0, 0, tiled=True)

    def transpose(field):
        return lax.all_to_all(field, frame_axes, 0, 0, tiled=True)

    def swap(field, axis):
        return lax.ppermute(field, axis, [(0, 1), (1, 0)])

    def reduce_weights(keep, give):
        taken = swap(give, "core")
        (partial,) = call(k_weights, [((D, 2 * D), BF16)], order, keep, taken)
        parts = lax.all_to_all(partial.reshape(dp, D // dp, 2 * D), "dp", 0, 0, tiled=True)
        rows = D // dp // (z * xl)
        (summed,) = call(k_sum, [((z * xl, rows, 2 * D), BF16)], parts)
        parts = lax.all_to_all(summed, ("z", "xl"), 0, 0, tiled=True)
        (summed,) = call(k_sum, [((rows, 2 * D), BF16)], parts)
        total = (summed.astype(F32) + swap(summed, "view").astype(F32)).astype(BF16)
        rows = rows // 2
        first = place[1] == 0
        mine = jnp.where(first, total[:rows], total[rows:])
        other = swap(jnp.where(first, total[rows:], total[:rows]), "core")
        low, high = jnp.where(first, mine, other), jnp.where(first, other, mine)
        return jnp.concatenate([low, high[:, :D]], axis=1), high[:, D:]

    views = VIEWS // 2
    x_keep, og_keep, send, st1 = call(
        k_split, [half16, half16, ((HALF, 2 * D), BF16), stats],
        level_in.reshape(views, 2 * PX, D), out_grad.reshape(views, 2 * PX, D), place=place,
    )
    recv = swap(send, "view")
    stream, packed_one, mixed_one, normed_one, og, own, st2 = call(
        functools.partial(k_view, entries),
        [tok32, ((T, 3 * D), BF16), tok16, tok32, tok16, ((2 * VIEWS, 128), F32), stats],
        x_keep, og_keep, recv, share(st1), view_qkv, view_out, place=place,
    )
    out_field, normed_two, inverse_two = call(
        functools.partial(k_norm_two, entries), [moved, tok32, ((VIEWS, 128), F32)], stream, og, share(st2)
    )
    back, keep_two, give_two = call(
        k_time, [moved, wide, wide], transpose(out_field), time_qkv, time_out, place=place
    )
    o_keep, o_send, ghid, st3 = call(
        k_level_out, [half16, half16, tok16, stats], transpose(back), stream, normed_two, place=place
    )
    o_recv = swap(o_send, "view")
    u_keep, u_send, keep_one, give_one, sums_two, st4 = call(
        functools.partial(k_view_back, entries),
        [half32, half16, wide, wide, ((2 * VIEWS, 128), F32), stats],
        ghid, normed_two, inverse_two, share(st3), og, packed_one, mixed_one, normed_one, own,
        view_qkv, view_out, place=place,
    )
    u_recv = swap(u_send, "view")
    level_out, level_in_grad, sums = call(
        functools.partial(k_finish, entries),
        [((views, 2 * PX, D), BF16), ((views, 2 * PX, D), BF16), ((4, views, 128), F32)],
        share(st4), sums_two, own, x_keep, send, u_keep, u_recv, o_keep, o_recv, place=place,
    )
    time_qkv_grad, time_out_grad = reduce_weights(keep_two, give_two)
    view_qkv_grad, view_out_grad = reduce_weights(keep_one, give_one)
    return (
        level_out.reshape(level_in.shape),
        level_in_grad.reshape(level_in.shape),
        view_qkv_grad,
        view_out_grad,
        time_qkv_grad,
        time_out_grad,
        sums[:, :, :GROUPS].reshape(2, 2, views, 1, GROUPS),
    )


def solution(mesh):
    frames, dp = mesh.shape["frame"], mesh.shape["dp"]
    sizes = (frames // 4, 2, 2, dp)
    fine = Mesh(mesh.devices.reshape((2,) + sizes), ("view", "z", "xl", "core", "dp"))
    split = ("z", "xl", "core")
    tokens = P("view", split, "dp", None)
    rows = P(split + ("dp",), None)
    return jax.shard_map(
        functools.partial(body, sizes),
        mesh=fine,
        in_specs=(tokens, tokens, P(), P(), P(), P()),
        out_specs=(tokens, tokens, rows, rows, rows, rows, P(None, None, "view", split, None)),
        check_vma=False,
    )
```

```python
import functools

import jax
import jax.numpy as jnp
import numpy as np
from jax import lax
from jax.experimental import pallas as pl
from jax.experimental.pallas import tpu as pltpu
from jax.sharding import Mesh, PartitionSpec as P

HEADS = 10
HD = 64
GROUPS = 32
EPS = 1e-05
D = 640
CH = D // GROUPS
VIEWS = 8
PX = 16
T = VIEWS * PX
HALF = T // 2
SCALE = HD ** (-0.5)
F32 = jnp.float32
BF16 = jnp.bfloat16
VMEM_LIMIT = 32


def group_matrix():
    row = lax.broadcasted_iota(jnp.int32, (D, 128), 0)
    low = lax.broadcasted_iota(jnp.int32, (D, 128), 1) * CH
    return ((row >= low) & (row < low + CH)).astype(F32).astype(BF16)


def three_parts(rows):
    high = rows.astype(BF16)
    rest = rows - high.astype(F32)
    middle = rest.astype(BF16)
    return high, middle, (rest - middle.astype(F32)).astype(BF16)


def exact_product(rows, member, dims):
    count = rows.shape[0]
    stacked = jnp.concatenate([part.astype(F32) for part in three_parts(rows)], axis=0).astype(BF16)
    out = lax.dot_general(stacked, member, (dims, ((), ())), preferred_element_type=F32)
    return out[:count] + (out[count : 2 * count] + out[2 * count :])


def to_groups(rows, member):
    return exact_product(rows, member, ((1,), (0,)))


def to_channels(groups, member):
    return exact_product(groups, member, ((1,), (1,)))


def both_sums(grad, normed, member):
    return to_groups(jnp.concatenate([view_sum(grad), view_sum(grad * normed)], axis=0), member)


def view_sum(tokens):
    return jnp.sum(tokens.reshape(tokens.shape[0] // PX, PX, D), axis=1)


def per_token(rows):
    return jnp.broadcast_to(rows[:, None, :], (rows.shape[0], PX, D)).reshape(rows.shape[0] * PX, D)


def partial_stats(tokens, member):
    mean = to_groups(view_sum(tokens), member) * (1.0 / (PX * CH))
    centred = tokens - per_token(to_channels(mean, member))
    return jnp.concatenate([mean, to_groups(view_sum(centred * centred), member)], axis=0)


def merge_stats(means, spreads, entries):
    count = len(means)
    mean = sum(means) * (1.0 / count)
    spread = sum(spreads)
    for other in means:
        gap = other - mean
        spread = spread + gap * gap * float(PX * CH)
    return mean, lax.rsqrt(spread * (1.0 / entries) + EPS)


def spread_out(ref, both):
    ref[...] = jnp.broadcast_to(both[None], ref.shape)


def mm(left, right):
    return jnp.dot(left, right, preferred_element_type=F32)


def mm_t(left, right):
    return lax.dot_general(left, right, (((1,), (1,)), ((), ())), preferred_element_type=F32)


def t_mm(left, right):
    return lax.dot_general(left, right, (((0,), (0,)), ((), ())), preferred_element_type=F32)


def lane_low(rows):
    return lax.broadcasted_iota(jnp.int32, (rows, 128), 1) < HD


def both_heads(pair):
    low = lane_low(pair.shape[0])
    zero = jnp.zeros_like(pair)
    return jnp.concatenate([jnp.where(low, pair, zero), jnp.where(low, zero, pair)], axis=0)


def join_heads(stacked):
    return jnp.where(lane_low(T), stacked[:T], stacked[T:])


def same_sequence(period):
    row = lax.broadcasted_iota(jnp.int32, (2 * T, T), 0)
    col = lax.broadcasted_iota(jnp.int32, (2 * T, T), 1)
    return ((row ^ col) & (period - 1)) == 0


def softmax_pair(stacked_q, keys, allowed):
    scores = jnp.where(allowed, mm_t(stacked_q, keys) * SCALE, -1e30)
    top = jnp.max(scores, axis=-1, keepdims=True)
    weights = jnp.exp(scores - top)
    return weights / jnp.sum(weights, axis=-1, keepdims=True)


def pair_of(index):
    return slice(index * 128, (index + 1) * 128)


def attend(packed, allowed):
    outs = []
    for pair in range(HEADS // 2):
        q = both_heads(packed[:, pair_of(pair)])
        k = packed[:, pair_of(pair + 5)]
        v = packed[:, pair_of(pair + 10)]
        prob = softmax_pair(q, k, allowed).astype(BF16)
        outs.append(join_heads(mm(prob, v)).astype(BF16))
    return jnp.concatenate(outs, axis=1)


def attend_back(grad, packed, allowed):
    dqs, dks, dvs = [], [], []
    for pair in range(HEADS // 2):
        q = both_heads(packed[:, pair_of(pair)])
        k = packed[:, pair_of(pair + 5)]
        v = packed[:, pair_of(pair + 10)]
        g = both_heads(grad[:, pair_of(pair)])
        prob = softmax_pair(q, k, allowed)
        dvs.append(t_mm(prob.astype(BF16), g).astype(BF16))
        dprob = mm_t(g, v)
        dscore = prob * (dprob - jnp.sum(dprob * prob, axis=-1, keepdims=True))
        dscore = (dscore * SCALE).astype(BF16)
        dqs.append(join_heads(mm(dscore, k)).astype(BF16))
        dks.append(t_mm(dscore, q).astype(BF16))
    return jnp.concatenate(dqs + dks + dvs, axis=1)


def halves(ref, first):
    low = ref[:, 0, 0:PX, :].reshape(HALF, D)
    high = ref[:, 0, PX : 2 * PX, :].reshape(HALF, D)
    return jnp.where(first, low, high), jnp.where(first, high, low)


def regrouped(own_ref, other_ref, first):
    mine, theirs = halves(own_ref, first)[0], halves(other_ref, first)[0]
    return jnp.concatenate([jnp.where(first, mine, theirs), jnp.where(first, theirs, mine)], axis=0)


def k_first_stats(place, x_ref, stats_ref):
    keep, give = halves(x_ref, place[0] == 0)
    tokens = jnp.concatenate([keep, give], axis=0).astype(F32)
    spread_out(stats_ref, partial_stats(tokens, group_matrix()))


def normalized(x, rows, member):
    channels = to_channels(rows, member)
    return (x - per_token(channels[:VIEWS])) * per_token(channels[VIEWS:])


def k_view(entries, place, x_ref, other_ref, g_ref, wqkv_ref, wout_ref, stream_ref, saved_ref, own_ref, stats_ref):
    first = place[0] == 0
    member = group_matrix()
    sources = g_ref.shape[0]
    half = VIEWS // 2

    def side(low):
        chosen = range(low, low + sources // 2)
        means = [g_ref[s, a * half : (a + 1) * half, :] for s in chosen for a in range(2)]
        spreads = [g_ref[s, VIEWS + a * half : VIEWS + (a + 1) * half, :] for s in chosen for a in range(2)]
        return merge_stats(means, spreads, entries)

    low, high = side(0), side(sources // 2)
    rows = jnp.concatenate([low[0], high[0], low[1], high[1]], axis=0)
    own_ref[...] = rows
    x = regrouped(x_ref, other_ref, first).astype(F32)
    packed = mm(normalized(x, rows, member).astype(BF16), wqkv_ref[...]).astype(BF16)
    saved_ref[:, : 3 * D] = packed
    mixed = attend(packed, same_sequence(PX))
    saved_ref[:, 3 * D :] = mixed
    stream = x + mm(mixed, wout_ref[...])
    stream_ref[...] = stream
    spread_out(stats_ref, partial_stats(stream, member))


def k_norm_two(entries, place, stream_ref, grad_ref, other_ref, g_ref, send_ref, rows_ref):
    member = group_matrix()
    sources = range(g_ref.shape[0])
    mean, inverse = merge_stats(
        [g_ref[s, 0:VIEWS, :] for s in sources], [g_ref[s, VIEWS:, :] for s in sources], entries
    )
    rows = jnp.concatenate([mean, inverse], axis=0)
    rows_ref[...] = rows
    shape = send_ref.shape[:2] + (D,)
    send_ref[:, :, :D] = normalized(stream_ref[...], rows, member).astype(BF16).reshape(shape)
    send_ref[:, :, D:] = regrouped(grad_ref, other_ref, place[0] == 0).reshape(shape)


def weight_sides(core, hidden, mixed, packed_grad, grad, keep_ref, give_ref):
    first = core == 0
    quarter = packed_grad[:, :D], packed_grad[:, D : 2 * D], packed_grad[:, 2 * D :], grad
    keep_ref[:, :D] = hidden
    give_ref[:, :D] = hidden
    keep_ref[:, D : 2 * D] = jnp.where(first, hidden, mixed)
    give_ref[:, D : 2 * D] = jnp.where(first, mixed, hidden)
    for slot in range(2):
        cols = slice((2 + slot) * D, (3 + slot) * D)
        keep_ref[:, cols] = jnp.where(first, quarter[slot], quarter[2 + slot])
        give_ref[:, cols] = jnp.where(first, quarter[2 + slot], quarter[slot])


def k_time(place, recv_ref, wqkv_ref, wout_ref, back_ref, keep_ref, give_ref):
    hidden = recv_ref[:, :, :D].reshape(T, D)
    grad = recv_ref[:, :, D:].reshape(T, D)
    allowed = same_sequence(recv_ref.shape[1])
    packed = mm(hidden, wqkv_ref[...]).astype(BF16)
    mixed = attend(packed, allowed)
    shape = back_ref.shape[:2] + (D,)
    back_ref[:, :, :D] = mm(mixed, wout_ref[...]).astype(BF16).reshape(shape)
    packed_grad = attend_back(mm_t(grad, wout_ref[...]).astype(BF16), packed, allowed)
    back_ref[:, :, D:] = mm_t(packed_grad, wqkv_ref[...]).astype(BF16).reshape(shape)
    weight_sides(place[1], hidden, mixed, packed_grad, grad, keep_ref, give_ref)


def k_back_stats(back_ref, stream_ref, rows_ref, stats_ref):
    member = group_matrix()
    normed = normalized(stream_ref[...], rows_ref[...], member)
    grad = back_ref[:, :, D:].reshape(T, D).astype(F32)
    spread_out(stats_ref, both_sums(grad, normed, member))


def k_view_back(entries, place, back_ref, stream_ref, rows_ref, g_ref, og_ref, ogother_ref, x_ref, other_ref, own_ref,
                saved_ref, wout_ref, keep_ref, give_ref, pgrad_ref, stream_grad_ref, normed_ref, sums_ref):
    first = place[0] == 0
    member = group_matrix()
    sums = g_ref[0]
    for s in range(1, g_ref.shape[0]):
        sums = sums + g_ref[s]
    sums_ref[...] = sums
    channels = to_channels(jnp.concatenate([sums * (1.0 / entries), rows_ref[...], own_ref[...]], axis=0), member)
    m1, m2, mean, inverse, mean_one, inverse_one = (
        per_token(channels[k * VIEWS : (k + 1) * VIEWS]) for k in range(6)
    )
    normed_two = (stream_ref[...] - mean) * inverse
    ghid = back_ref[:, :, D:].reshape(T, D).astype(F32)
    grad_stream = regrouped(og_ref, ogother_ref, first).astype(F32) + inverse * (ghid - m1 - normed_two * m2)
    stream_grad_ref[...] = grad_stream
    grad_b = grad_stream.astype(BF16)
    packed_grad = attend_back(mm_t(grad_b, wout_ref[...]).astype(BF16), saved_ref[:, : 3 * D], same_sequence(PX))
    pgrad_ref[...] = packed_grad
    normed = (regrouped(x_ref, other_ref, first).astype(F32) - mean_one) * inverse_one
    normed_ref[...] = normed
    weight_sides(place[1], normed.astype(BF16), saved_ref[:, 3 * D :], packed_grad, grad_b, keep_ref, give_ref)


def k_view_stats(place, pgrad_ref, stream_grad_ref, back_ref, stream_ref, none_ref, own_ref, wqkv_ref,
                 ukeep_ref, okeep_ref, send_ref, stats_ref):
    first = place[0] == 0
    member = group_matrix()
    grad = mm_t(pgrad_ref[...], wqkv_ref[...]).astype(BF16).astype(F32)
    stats = both_sums(grad, none_ref[...], member)
    stats_ref[...] = stats
    partly = stream_grad_ref[...] + per_token(to_channels(own_ref[VIEWS:, :], member)) * grad
    temporal = back_ref[:, :, :D].reshape(T, D).astype(F32)
    out = (stream_ref[...] + temporal).astype(BF16)
    ukeep_ref[...] = jnp.where(first, partly[:HALF], partly[HALF:])
    okeep_ref[...] = jnp.where(first, out[:HALF], out[HALF:])
    send_ref[:, :D] = jnp.where(first, partly[HALF:], partly[:HALF]).astype(BF16)
    send_ref[:, D:] = jnp.where(first, out[HALF:], out[:HALF])


def k_finish(entries, place, g_ref, sumstwo_ref, own_ref, x_ref, ukeep_ref, okeep_ref, recv_ref,
             out_ref, grad_ref, sums_ref):
    first = place[0] == 0
    member = group_matrix()
    half = VIEWS // 2
    sums = g_ref[...]

    def mine(rows):
        return jnp.where(first, rows[:half], rows[half:])

    s1, s2 = mine(sums[:VIEWS]), mine(sums[VIEWS:])
    sums_ref[0] = s1
    sums_ref[1] = s2
    sums_ref[2] = mine(sumstwo_ref[0:VIEWS, :])
    sums_ref[3] = mine(sumstwo_ref[VIEWS:, :])
    inverse = mine(own_ref[VIEWS:, :])
    scale = inverse * (1.0 / entries)
    rows = jnp.concatenate([mine(own_ref[0:VIEWS, :]), inverse, s1 * scale, s2 * scale], axis=0)
    channels = to_channels(rows, member)
    mean_c, inverse_c, a, b = (per_token(channels[k * half : (k + 1) * half]) for k in range(4))

    def finished(part, x):
        normed = (x.astype(F32) - mean_c) * inverse_c
        return (part.astype(F32) - a - normed * b).astype(BF16)

    x_keep, x_give = halves(x_ref, first)
    keep = finished(ukeep_ref[...], x_keep)
    other = finished(recv_ref[:, :D], x_give)
    shape = (half, PX, D)
    grad_ref[:, 0:PX, :] = jnp.where(first, keep, other).reshape(shape)
    grad_ref[:, PX:, :] = jnp.where(first, other, keep).reshape(shape)
    okeep, orecv = okeep_ref[...], recv_ref[:, D:]
    out_ref[:, 0:PX, :] = jnp.where(first, okeep, orecv).reshape(shape)
    out_ref[:, PX:, :] = jnp.where(first, orecv, okeep).reshape(shape)


def added32(*refs):
    total = refs[0][...].astype(F32)
    for ref in refs[1:]:
        total = total + ref[...].astype(F32)
    return total


def added(*refs):
    return added32(*refs).astype(BF16)


def split_rows(total, refs, cols=slice(None)):
    rows = total.shape[0] // len(refs)
    for s, ref in enumerate(refs):
        ref[:, cols] = total[s * rows : (s + 1) * rows]


def weight_tile(unit, places, keep_ref, recv_ref):
    row = lax.broadcasted_iota(jnp.int32, (D, D), 0)
    left = jnp.concatenate([keep_ref[:, unit * D : (unit + 1) * D], recv_ref[:, unit * D : (unit + 1) * D]], axis=0)
    cols = slice((2 + unit) * D, (3 + unit) * D)
    right = jnp.concatenate([keep_ref[:, cols], recv_ref[:, cols]], axis=0)
    order = (row == places).astype(BF16)
    return t_mm(mm(left, order).astype(BF16), right).astype(BF16)


def k_weights_time(place, table_ref, keep_ref, recv_ref, *out_refs):
    places = table_ref[place[2]]
    for unit in range(2):
        split_rows(weight_tile(unit, places, keep_ref, recv_ref), out_refs, slice(unit * D, (unit + 1) * D))


def k_weights_view(table_ref, keep_ref, recv_ref, out_ref):
    places = table_ref[table_ref.shape[0] - 1]
    for unit in range(2):
        out_ref[:, unit * D : (unit + 1) * D] = weight_tile(unit, places, keep_ref, recv_ref)


def k_sum_time(*refs):
    split_rows(added(*refs[:4]), refs[4:])


def k_sum_rows(parts_ref, *refs):
    times, out_ref = refs[:4], refs[4]
    chips = out_ref.shape[0]
    rows = times[0].shape[0]
    count = parts_ref.shape[0] // rows
    view = sum(parts_ref[s * rows : (s + 1) * rows, :].astype(F32) for s in range(count))
    time = added32(*times)
    units = [view[:, :D], view[:, D:], time[:, :D], time[:, D:]]
    for row in range(out_ref.shape[2] // D):
        block = jnp.stack([unit[row * chips : (row + 1) * chips] for unit in units], axis=1)
        out_ref[:, :, row * D : (row + 1) * D] = block.astype(BF16)


def k_sum(parts_ref, out_ref):
    total = parts_ref[0].astype(F32)
    for s in range(1, parts_ref.shape[0]):
        total = total + parts_ref[s].astype(F32)
    out_ref[...] = total.astype(BF16)


def k_rows(place, near_ref, far_ref, vqkv_ref, vout_ref, tqkv_ref, tout_ref):
    both = jnp.where(place[0] == place[1], near_ref[...].astype(F32), far_ref[...].astype(F32))
    low, high = both[:4], both[4:]
    for row in range(vout_ref.shape[0]):
        cols = slice(row * D, (row + 1) * D)
        line = slice(row, row + 1)
        for unit, qkv_ref, out_ref in ((0, vqkv_ref, vout_ref), (2, tqkv_ref, tout_ref)):
            qkv_ref[line, :D] = low[unit : unit + 1, cols].astype(BF16)
            qkv_ref[line, D : 2 * D] = low[unit + 1 : unit + 2, cols].astype(BF16)
            qkv_ref[line, 2 * D :] = high[unit : unit + 1, cols].astype(BF16)
            out_ref[line, :] = high[unit + 1 : unit + 2, cols].astype(BF16)


def call(kernel, outs, *args, place=None, us=2, vmem=VMEM_LIMIT):
    specs = [pl.BlockSpec(memory_space=pltpu.VMEM)] * len(args)
    if place is not None:
        specs = [pl.BlockSpec(memory_space=pltpu.SMEM)] + specs
        args = (place,) + args
    return pl.pallas_call(
        kernel,
        out_shape=[jax.ShapeDtypeStruct(shape, dtype) for shape, dtype in outs],
        in_specs=specs,
        out_specs=[pl.BlockSpec(memory_space=pltpu.VMEM)] * len(outs),
        compiler_params=pltpu.CompilerParams(vmem_limit_bytes=vmem * 1024 * 1024),
        cost_estimate=pl.CostEstimate(flops=int(us * 1e9), bytes_accessed=int(us * 3e6), transcendentals=0),
    )(*args)


def row_table(z, xl, core, dp):
    rows = D // (z * xl * core * dp)
    ring = core * xl
    chip = np.arange(z).reshape(1, 1, 1, z)
    row = np.arange(rows).reshape(1, 1, rows, 1)

    def place(y, x):
        return ((((chip * xl + x % xl) * core + x // xl) * dp + y) * rows + row).reshape(1, -1)

    table = []
    for me_x in range(ring):
        for me_dp in range(dp):
            y, x = (me_dp + np.arange(dp)) % dp, (me_x + np.arange(ring)) % ring
            table.append(place(y.reshape(dp, 1, 1, 1), x.reshape(1, ring, 1, 1)))
    table.append(place(np.arange(dp).reshape(1, dp, 1, 1), np.arange(ring).reshape(ring, 1, 1, 1)))
    return np.stack(table).astype(np.int32)


def body(sizes, level_in, out_grad, view_qkv, view_out, time_qkv, time_out):
    z, xl, core, dp = sizes
    frames = z * xl * core
    entries = float(dp * 2 * PX * CH)
    frame_axes = ("z", "xl", "core")
    mates = ("view", "dp")
    group = 2 * dp
    spot = (lax.axis_index("view") * xl + lax.axis_index("xl")) * dp + lax.axis_index("dp")
    place = jnp.stack([lax.axis_index("view"), lax.axis_index("core"), spot]).astype(jnp.int32)
    table = jnp.asarray(row_table(z, xl, core, dp))
    rows = D // (z * xl * core * dp)
    stats = ((group, 2 * VIEWS, 128), F32)
    tok32, tok16 = ((T, D), F32), ((T, D), BF16)
    half32, half16 = ((HALF, D), F32), ((HALF, D), BF16)
    wide = ((T, 4 * D), BF16)
    moved = ((frames, T // frames, 2 * D), BF16)

    def share(field):
        return lax.all_to_all(field, mates, 0, 0, tiled=True)

    def transpose(field):
        return lax.all_to_all(field, frame_axes, 0, 0, tiled=True)

    def swap(field, axis):
        return lax.ppermute(field, axis, [(0, 1), (1, 0)])

    def shifted(pieces, axis):
        return [
            lax.ppermute(piece, axis, [(i, (i + step + 1) % 4) for i in range(4)]) for step, piece in enumerate(pieces)
        ]

    def crossed(field, step):
        return field + lax.ppermute(field, "dp", [(i, i ^ step) for i in range(dp)])

    views = VIEWS // 2
    rows16 = ((2 * VIEWS, 128), F32)
    x_other, og_other = swap(level_in, "view"), swap(out_grad, "view")
    (st1,) = call(k_first_stats, [stats], level_in, place=place)
    stream, saved, own, st2 = call(
        functools.partial(k_view, entries), [tok32, wide, rows16, stats],
        level_in, x_other, share(st1), view_qkv, view_out, place=place, us=4,
    )
    out_field, rows_two = call(
        functools.partial(k_norm_two, entries), [moved, rows16], stream, out_grad, og_other, share(st2), place=place
    )
    back, keep_two, give_two = call(
        k_time, [moved, wide, wide], transpose(out_field), time_qkv, time_out, place=place, us=6
    )
    mine, *pieces = call(
        k_weights_time, [((D // 4, 2 * D), BF16)] * 4, table, keep_two, swap(give_two, "core"), place=place, us=3
    )
    moved_back, _ = lax.optimization_barrier((transpose(back), pieces))
    time_parts = [mine, *shifted(pieces, "dp")]
    (st3,) = call(k_back_stats, [stats], moved_back, stream, rows_two, us=1)
    shared, time_parts = lax.optimization_barrier((share(st3), time_parts))
    keep_one, give_one, pgrad, stream_grad, normed_one, sums_two = call(
        functools.partial(k_view_back, entries), [wide, wide, ((T, 3 * D), BF16), tok32, tok32, rows16],
        moved_back, stream, rows_two, shared, out_grad, og_other, level_in, x_other, own, saved, view_out,
        place=place, us=5,
    )
    u_keep, o_keep, send_back, st4 = call(
        k_view_stats, [half32, half16, ((HALF, 2 * D), BF16), rows16],
        pgrad, stream_grad, moved_back, stream, normed_one, own, view_qkv, place=place, us=3,
    )
    taken, st4 = lax.optimization_barrier((swap(give_one, "core"), st4))
    (partial,) = call(k_weights_view, [((D, 2 * D), BF16)], table, keep_one, taken, place=None, us=3)
    time_parts, partial = lax.optimization_barrier((time_parts, partial))
    parts = lax.all_to_all(partial, ("view", "xl", "dp"), 0, 0, tiled=True)
    mine, *pieces = call(k_sum_time, [((D // 16, 2 * D), BF16)] * 4, *time_parts)
    time_parts = [mine, *shifted(pieces, ("view", "xl"))]
    parts, time_parts, st4 = lax.optimization_barrier((parts, time_parts, st4 + swap(st4, "view")))
    (by_z,) = call(k_sum_rows, [((z, 4, rows * D), BF16)], parts, *time_parts)
    by_z, st4, send_back = lax.optimization_barrier((by_z, st4, send_back))
    by_z = lax.all_to_all(by_z, "z", 0, 0, tiled=True)
    recv_back = swap(send_back, "view")
    st4 = crossed(crossed(st4, 1), 2)
    by_z, st4 = lax.optimization_barrier((by_z, st4))
    (summed,) = call(k_sum, [((4, rows * D), BF16)], by_z)
    level_out, level_in_grad, sums = call(
        functools.partial(k_finish, entries),
        [((views, 2 * PX, D), BF16), ((views, 2 * PX, D), BF16), ((4, views, 128), F32)],
        st4, sums_two, own, level_in, u_keep, o_keep, recv_back, place=place, us=3,
    )
    first = place[1] == 0
    near = swap(summed, "core")
    pair = jnp.concatenate([jnp.where(first, summed, near), jnp.where(first, near, summed)], axis=0)
    qkv_row, out_row = ((rows, 3 * D), BF16), ((rows, D), BF16)
    view_qkv_grad, view_out_grad, time_qkv_grad, time_out_grad = call(
        k_rows, [qkv_row, out_row, qkv_row, out_row], pair, swap(pair, "view"), place=place
    )
    return (
        level_out.reshape(level_in.shape),
        level_in_grad.reshape(level_in.shape),
        view_qkv_grad,
        view_out_grad,
        time_qkv_grad,
        time_out_grad,
        sums[:, :, :GROUPS].reshape(2, 2, views, 1, GROUPS),
    )


def solution(mesh):
    frames, dp = mesh.shape["frame"], mesh.shape["dp"]
    sizes = (frames // 4, 2, 2, dp)
    fine = Mesh(mesh.devices.reshape((2,) + sizes), ("view", "z", "xl", "core", "dp"))
    split = ("z", "xl", "core")
    tokens = P("view", split, "dp", None)
    rows = P(split + ("dp",), None)
    return jax.shard_map(
        functools.partial(body, sizes),
        mesh=fine,
        in_specs=(tokens, tokens, P(), P(), P(), P()),
        out_specs=(tokens, tokens, rows, rows, rows, rows, P(None, None, "view", split, None)),
        check_vma=False,
    )
```

```python
import functools

import jax
import jax.numpy as jnp
import numpy as np
from jax import lax
from jax.experimental import pallas as pl
from jax.experimental.pallas import tpu as pltpu
from jax.sharding import Mesh, PartitionSpec as P

HEADS = 10
HD = 64
GROUPS = 32
EPS = 1e-05
D = 640
CH = D // GROUPS
VIEWS = 8
PX = 16
T = VIEWS * PX
HALF = T // 2
SCALE = HD ** (-0.5)
F32 = jnp.float32
BF16 = jnp.bfloat16
VMEM_LIMIT = 32


def group_matrix():
    row = lax.broadcasted_iota(jnp.int32, (D, 128), 0)
    low = lax.broadcasted_iota(jnp.int32, (D, 128), 1) * CH
    return ((row >= low) & (row < low + CH)).astype(F32).astype(BF16)


def three_parts(rows):
    high = rows.astype(BF16)
    rest = rows - high.astype(F32)
    middle = rest.astype(BF16)
    return high, middle, (rest - middle.astype(F32)).astype(BF16)


def exact_product(rows, member, dims):
    count = rows.shape[0]
    stacked = jnp.concatenate([part.astype(F32) for part in three_parts(rows)], axis=0).astype(BF16)
    out = lax.dot_general(stacked, member, (dims, ((), ())), preferred_element_type=F32)
    return out[:count] + (out[count : 2 * count] + out[2 * count :])


def to_groups(rows, member):
    return exact_product(rows, member, ((1,), (0,)))


def to_channels(groups, member):
    return exact_product(groups, member, ((1,), (1,)))


def both_sums(grad, normed, member):
    return to_groups(jnp.concatenate([view_sum(grad), view_sum(grad * normed)], axis=0), member)


def view_sum(tokens):
    return jnp.sum(tokens.reshape(tokens.shape[0] // PX, PX, D), axis=1)


def per_token(rows):
    return jnp.broadcast_to(rows[:, None, :], (rows.shape[0], PX, D)).reshape(rows.shape[0] * PX, D)


def partial_stats(tokens, member):
    mean = to_groups(view_sum(tokens), member) * (1.0 / (PX * CH))
    centred = tokens - per_token(to_channels(mean, member))
    return jnp.concatenate([mean, to_groups(view_sum(centred * centred), member)], axis=0)


def merge_stats(means, spreads, entries):
    count = len(means)
    mean = sum(means) * (1.0 / count)
    spread = sum(spreads)
    for other in means:
        gap = other - mean
        spread = spread + gap * gap * float(PX * CH)
    return mean, lax.rsqrt(spread * (1.0 / entries) + EPS)


def spread_out(ref, both):
    ref[...] = jnp.broadcast_to(both[None], ref.shape)


def mm(left, right):
    return jnp.dot(left, right, preferred_element_type=F32)


def mm_t(left, right):
    return lax.dot_general(left, right, (((1,), (1,)), ((), ())), preferred_element_type=F32)


def t_mm(left, right):
    return lax.dot_general(left, right, (((0,), (0,)), ((), ())), preferred_element_type=F32)


def lane_low(rows):
    return lax.broadcasted_iota(jnp.int32, (rows, 128), 1) < HD


def both_heads(pair):
    low = lane_low(pair.shape[0])
    zero = jnp.zeros_like(pair)
    return jnp.concatenate([jnp.where(low, pair, zero), jnp.where(low, zero, pair)], axis=0)


def join_heads(stacked):
    return jnp.where(lane_low(T), stacked[:T], stacked[T:])


def same_sequence(period):
    row = lax.broadcasted_iota(jnp.int32, (2 * T, T), 0)
    col = lax.broadcasted_iota(jnp.int32, (2 * T, T), 1)
    return ((row ^ col) & (period - 1)) == 0


def softmax_all(stacked_q, keys, allowed):
    scores = jnp.concatenate([mm_t(q, k) for q, k in zip(stacked_q, keys)], axis=0)
    allowed = jnp.concatenate([allowed] * len(keys), axis=0)
    scores = jnp.where(allowed, scores * SCALE, -1e30)
    top = jnp.max(scores, axis=-1, keepdims=True)
    weights = jnp.exp(scores - top)
    return weights * (1.0 / jnp.sum(weights, axis=-1, keepdims=True))


def pair_of(index):
    return slice(index * 128, (index + 1) * 128)


def pieces_of(packed, first):
    return [packed[:, pair_of(first + pair)] for pair in range(HEADS // 2)]


def rows_of(stacked, pair):
    return stacked[pair * 2 * T : (pair + 1) * 2 * T]


def attend(packed, allowed):
    q, k, v = [both_heads(piece) for piece in pieces_of(packed, 0)], pieces_of(packed, 5), pieces_of(packed, 10)
    prob = softmax_all(q, k, allowed)
    rounded = prob.astype(BF16)
    outs = [join_heads(mm(rows_of(rounded, pair), v[pair])).astype(BF16) for pair in range(HEADS // 2)]
    return jnp.concatenate(outs, axis=1), prob


def attend_back(grad, packed, allowed, prob=None):
    q, k, v = [both_heads(piece) for piece in pieces_of(packed, 0)], pieces_of(packed, 5), pieces_of(packed, 10)
    g = [both_heads(piece) for piece in pieces_of(grad, 0)]
    if prob is None:
        prob = softmax_all(q, k, allowed)
    rounded = prob.astype(BF16)
    dprob = jnp.concatenate([mm_t(x, y) for x, y in zip(g, v)], axis=0)
    dscore = prob * (dprob - jnp.sum(dprob * prob, axis=-1, keepdims=True))
    dscore = (dscore * SCALE).astype(BF16)
    pairs = range(HEADS // 2)
    dvs = [t_mm(rows_of(rounded, pair), g[pair]).astype(BF16) for pair in pairs]
    dqs = [join_heads(mm(rows_of(dscore, pair), k[pair])).astype(BF16) for pair in pairs]
    dks = [t_mm(rows_of(dscore, pair), q[pair]).astype(BF16) for pair in pairs]
    return jnp.concatenate(dqs + dks + dvs, axis=1)


def halves(ref, first):
    low = ref[:, 0, 0:PX, :].reshape(HALF, D)
    high = ref[:, 0, PX : 2 * PX, :].reshape(HALF, D)
    return jnp.where(first, low, high), jnp.where(first, high, low)


def regrouped(own_ref, other_ref, first):
    mine, theirs = halves(own_ref, first)[0], halves(other_ref, first)[0]
    return jnp.concatenate([jnp.where(first, mine, theirs), jnp.where(first, theirs, mine)], axis=0)


def k_first_stats(place, x_ref, stats_ref):
    keep, give = halves(x_ref, place[0] == 0)
    tokens = jnp.concatenate([keep, give], axis=0).astype(F32)
    spread_out(stats_ref, partial_stats(tokens, group_matrix()))


def normalized(x, rows, member):
    channels = to_channels(rows, member)
    return (x - per_token(channels[:VIEWS])) * per_token(channels[VIEWS:])


def k_view(entries, place, x_ref, other_ref, g_ref, wqkv_ref, wout_ref, stream_ref, saved_ref, sides_ref, own_ref, stats_ref):
    first = place[0] == 0
    member = group_matrix()
    sources = g_ref.shape[0]
    half = VIEWS // 2

    def side(low):
        chosen = range(low, low + sources // 2)
        means = [g_ref[s, a * half : (a + 1) * half, :] for s in chosen for a in range(2)]
        spreads = [g_ref[s, VIEWS + a * half : VIEWS + (a + 1) * half, :] for s in chosen for a in range(2)]
        return merge_stats(means, spreads, entries)

    low, high = side(0), side(sources // 2)
    rows = jnp.concatenate([low[0], high[0], low[1], high[1]], axis=0)
    own_ref[...] = rows
    x = regrouped(x_ref, other_ref, first).astype(F32)
    hidden = normalized(x, rows, member).astype(BF16)
    packed = mm(hidden, wqkv_ref[...]).astype(BF16)
    saved_ref[...] = packed
    mixed, _ = attend(packed, same_sequence(PX))
    sides_ref[:, :D] = hidden
    sides_ref[:, D:] = mixed
    stream = x + mm(mixed, wout_ref[...])
    stream_ref[...] = stream
    spread_out(stats_ref, partial_stats(stream, member))


def k_norm_two(entries, place, stream_ref, grad_ref, other_ref, g_ref, send_ref, rows_ref):
    member = group_matrix()
    sources = range(g_ref.shape[0])
    mean, inverse = merge_stats(
        [g_ref[s, 0:VIEWS, :] for s in sources], [g_ref[s, VIEWS:, :] for s in sources], entries
    )
    rows = jnp.concatenate([mean, inverse], axis=0)
    rows_ref[...] = rows
    shape = send_ref.shape[:2] + (D,)
    send_ref[:, :, :D] = normalized(stream_ref[...], rows, member).astype(BF16).reshape(shape)
    send_ref[:, :, D:] = regrouped(grad_ref, other_ref, place[0] == 0).reshape(shape)


def weight_sides(core, hidden, mixed, packed_grad, grad, keep_ref, give_ref):
    first = core == 0
    keep_ref[:, :D] = hidden
    give_ref[:, :D] = hidden
    keep_ref[:, D : 2 * D] = jnp.where(first, hidden, mixed)
    give_ref[:, D : 2 * D] = jnp.where(first, mixed, hidden)
    right_sides(core, packed_grad, grad, keep_ref, give_ref, 2 * D)


def right_sides(core, packed_grad, grad, keep_ref, give_ref, start=0):
    first = core == 0
    quarter = packed_grad[:, :D], packed_grad[:, D : 2 * D], packed_grad[:, 2 * D :], grad
    for slot in range(2):
        cols = slice(start + slot * D, start + (slot + 1) * D)
        keep_ref[:, cols] = jnp.where(first, quarter[slot], quarter[2 + slot])
        give_ref[:, cols] = jnp.where(first, quarter[2 + slot], quarter[slot])


def k_time(place, recv_ref, wqkv_ref, wout_ref, back_ref, keep_ref, give_ref):
    hidden = recv_ref[:, :, :D].reshape(T, D)
    grad = recv_ref[:, :, D:].reshape(T, D)
    allowed = same_sequence(recv_ref.shape[1])
    packed = mm(hidden, wqkv_ref[...]).astype(BF16)
    mixed, probs = attend(packed, allowed)
    shape = back_ref.shape[:2] + (D,)
    back_ref[:, :, :D] = mm(mixed, wout_ref[...]).astype(BF16).reshape(shape)
    packed_grad = attend_back(mm_t(grad, wout_ref[...]).astype(BF16), packed, allowed, probs)
    back_ref[:, :, D:] = mm_t(packed_grad, wqkv_ref[...]).astype(BF16).reshape(shape)
    weight_sides(place[1], hidden, mixed, packed_grad, grad, keep_ref, give_ref)


def k_back_stats(back_ref, stream_ref, rows_ref, stats_ref):
    member = group_matrix()
    grad = back_ref[:, :, D:].reshape(T, D).astype(F32)
    spread_out(stats_ref, both_sums(grad, normalized(stream_ref[...], rows_ref[...], member), member))


def k_view_back(entries, place, back_ref, stream_ref, rows_ref, g_ref, og_ref, ogother_ref, packed_ref, wout_ref,
                keep_ref, give_ref, pgrad_ref, stream_grad_ref, sums_ref):
    first = place[0] == 0
    member = group_matrix()
    sums = g_ref[0]
    for s in range(1, g_ref.shape[0]):
        sums = sums + g_ref[s]
    sums_ref[...] = sums
    channels = to_channels(jnp.concatenate([sums * (1.0 / entries), rows_ref[...]], axis=0), member)
    m1, m2, mean, inverse = (per_token(channels[k * VIEWS : (k + 1) * VIEWS]) for k in range(4))
    normed_two = (stream_ref[...] - mean) * inverse
    ghid = back_ref[:, :, D:].reshape(T, D).astype(F32)
    grad_stream = regrouped(og_ref, ogother_ref, first).astype(F32) + inverse * (ghid - m1 - normed_two * m2)
    stream_grad_ref[...] = grad_stream
    grad_b = grad_stream.astype(BF16)
    packed_grad = attend_back(mm_t(grad_b, wout_ref[...]).astype(BF16), packed_ref[...], same_sequence(PX))
    pgrad_ref[...] = packed_grad
    right_sides(place[1], packed_grad, grad_b, keep_ref, give_ref)


def k_view_stats(place, pgrad_ref, stream_grad_ref, back_ref, stream_ref, x_ref, other_ref, own_ref, wqkv_ref,
                 ukeep_ref, okeep_ref, send_ref, stats_ref):
    first = place[0] == 0
    member = group_matrix()
    grad = mm_t(pgrad_ref[...], wqkv_ref[...]).astype(BF16).astype(F32)
    channels = to_channels(own_ref[...], member)
    mean, inverse = per_token(channels[:VIEWS]), per_token(channels[VIEWS:])
    normed = (regrouped(x_ref, other_ref, first).astype(F32) - mean) * inverse
    stats_ref[...] = both_sums(grad, normed, member)
    partly = stream_grad_ref[...] + inverse * grad
    temporal = back_ref[:, :, :D].reshape(T, D).astype(F32)
    out = (stream_ref[...] + temporal).astype(BF16)
    ukeep_ref[...] = jnp.where(first, partly[:HALF], partly[HALF:])
    okeep_ref[...] = jnp.where(first, out[:HALF], out[HALF:])
    send_ref[:, :D] = jnp.where(first, partly[HALF:], partly[:HALF]).astype(BF16)
    send_ref[:, D:] = jnp.where(first, out[HALF:], out[:HALF])


def k_finish(entries, place, g_ref, sumstwo_ref, own_ref, x_ref, ukeep_ref, okeep_ref, recv_ref,
             out_ref, grad_ref, sums_ref):
    first = place[0] == 0
    member = group_matrix()
    half = VIEWS // 2
    sums = g_ref[...]

    def mine(rows):
        return jnp.where(first, rows[:half], rows[half:])

    s1, s2 = mine(sums[:VIEWS]), mine(sums[VIEWS:])
    sums_ref[0] = s1
    sums_ref[1] = s2
    sums_ref[2] = mine(sumstwo_ref[0:VIEWS, :])
    sums_ref[3] = mine(sumstwo_ref[VIEWS:, :])
    inverse = mine(own_ref[VIEWS:, :])
    scale = inverse * (1.0 / entries)
    rows = jnp.concatenate([mine(own_ref[0:VIEWS, :]), inverse, s1 * scale, s2 * scale], axis=0)
    channels = to_channels(rows, member)
    mean_c, inverse_c, a, b = (per_token(channels[k * half : (k + 1) * half]) for k in range(4))

    def finished(part, x):
        normed = (x.astype(F32) - mean_c) * inverse_c
        return (part.astype(F32) - a - normed * b).astype(BF16)

    x_keep, x_give = halves(x_ref, first)
    keep = finished(ukeep_ref[...], x_keep)
    other = finished(recv_ref[:, :D], x_give)
    shape = (half, PX, D)
    grad_ref[:, 0:PX, :] = jnp.where(first, keep, other).reshape(shape)
    grad_ref[:, PX:, :] = jnp.where(first, other, keep).reshape(shape)
    okeep, orecv = okeep_ref[...], recv_ref[:, D:]
    out_ref[:, 0:PX, :] = jnp.where(first, okeep, orecv).reshape(shape)
    out_ref[:, PX:, :] = jnp.where(first, orecv, okeep).reshape(shape)


def added32(*refs):
    total = refs[0][...].astype(F32)
    for ref in refs[1:]:
        total = total + ref[...].astype(F32)
    return total


def added(*refs):
    return added32(*refs).astype(BF16)


def split_rows(total, refs, cols=slice(None)):
    rows = total.shape[0] // len(refs)
    for s, ref in enumerate(refs):
        ref[:, cols] = total[s * rows : (s + 1) * rows]


def weight_tile(unit, places, keep_ref, recv_ref):
    row = lax.broadcasted_iota(jnp.int32, (D, D), 0)
    left = jnp.concatenate([keep_ref[:, unit * D : (unit + 1) * D], recv_ref[:, unit * D : (unit + 1) * D]], axis=0)
    cols = slice((2 + unit) * D, (3 + unit) * D)
    right = jnp.concatenate([keep_ref[:, cols], recv_ref[:, cols]], axis=0)
    order = (row == places).astype(BF16)
    return t_mm(mm(left, order).astype(BF16), right).astype(BF16)


def k_weights_time(place, table_ref, keep_ref, recv_ref, *out_refs):
    places = table_ref[place[2]]
    for unit in range(2):
        total = weight_tile(unit, places, keep_ref, recv_ref)
        split_rows(total, out_refs, slice(unit * D, (unit + 1) * D))


def k_left_sides(place, column_ref, mine_ref, theirs_ref, left_ref):
    first = place[1] == 0
    order = (lax.broadcasted_iota(jnp.int32, (D, D), 1) == column_ref[...]).astype(BF16)
    hidden = jnp.concatenate([mine_ref[:, :D], theirs_ref[:, :D]], axis=0)
    mixed = jnp.concatenate([mine_ref[:, D:], theirs_ref[:, D:]], axis=0)
    left_ref[0] = mm_t(order, hidden).astype(BF16)
    left_ref[1] = mm_t(order, jnp.where(first, hidden, mixed)).astype(BF16)


def k_weights_view(left_ref, mine_ref, theirs_ref, out_ref):
    for unit in range(2):
        cols = slice(unit * D, (unit + 1) * D)
        right = jnp.concatenate([mine_ref[:, cols], theirs_ref[:, cols]], axis=0)
        out_ref[:, cols] = mm(left_ref[unit], right).astype(BF16)


def k_sum_time(*refs):
    split_rows(added(*refs[:4]), refs[4:])


def k_sum_rows(parts_ref, *refs):
    times, out_ref = refs[:4], refs[4]
    chips = out_ref.shape[0]
    rows = times[0].shape[0]
    count = parts_ref.shape[0] // rows
    view = sum(parts_ref[s * rows : (s + 1) * rows, :].astype(F32) for s in range(count))
    time = added32(*times)
    units = [view[:, :D], view[:, D:], time[:, :D], time[:, D:]]
    for row in range(out_ref.shape[2] // D):
        block = jnp.stack([unit[row * chips : (row + 1) * chips] for unit in units], axis=1)
        out_ref[:, :, row * D : (row + 1) * D] = block.astype(BF16)


def k_sum(parts_ref, out_ref):
    total = parts_ref[0].astype(F32)
    for s in range(1, parts_ref.shape[0]):
        total = total + parts_ref[s].astype(F32)
    out_ref[...] = total.astype(BF16)


def k_rows(place, near_ref, far_ref, vqkv_ref, vout_ref, tqkv_ref, tout_ref):
    both = jnp.where(place[0] == place[1], near_ref[...].astype(F32), far_ref[...].astype(F32))
    low, high = both[:4], both[4:]
    for row in range(vout_ref.shape[0]):
        cols = slice(row * D, (row + 1) * D)
        line = slice(row, row + 1)
        for unit, qkv_ref, out_ref in ((0, vqkv_ref, vout_ref), (2, tqkv_ref, tout_ref)):
            qkv_ref[line, :D] = low[unit : unit + 1, cols].astype(BF16)
            qkv_ref[line, D : 2 * D] = low[unit + 1 : unit + 2, cols].astype(BF16)
            qkv_ref[line, 2 * D :] = high[unit : unit + 1, cols].astype(BF16)
            out_ref[line, :] = high[unit + 1 : unit + 2, cols].astype(BF16)


def call(kernel, outs, *args, place=None, us=2, vmem=VMEM_LIMIT):
    specs = [pl.BlockSpec(memory_space=pltpu.VMEM)] * len(args)
    if place is not None:
        specs = [pl.BlockSpec(memory_space=pltpu.SMEM)] + specs
        args = (place,) + args
    return pl.pallas_call(
        kernel,
        out_shape=[jax.ShapeDtypeStruct(shape, dtype) for shape, dtype in outs],
        in_specs=specs,
        out_specs=[pl.BlockSpec(memory_space=pltpu.VMEM)] * len(outs),
        compiler_params=pltpu.CompilerParams(vmem_limit_bytes=vmem * 1024 * 1024),
        cost_estimate=pl.CostEstimate(flops=int(us * 1e9), bytes_accessed=int(us * 3e6), transcendentals=0),
    )(*args)


def row_tables(z, xl, core, dp):
    rows = D // (z * xl * core * dp)
    ring = core * xl
    chip = np.arange(z).reshape(1, 1, 1, z)
    row = np.arange(rows).reshape(1, 1, rows, 1)

    def place(y, x):
        return ((((chip * xl + x % xl) * core + x // xl) * dp + y) * rows + row).reshape(1, -1)

    table = []
    for me_x in range(ring):
        for me_dp in range(dp):
            y, x = (me_dp + np.arange(dp)) % dp, (me_x + np.arange(ring)) % ring
            table.append(place(y.reshape(dp, 1, 1, 1), x.reshape(1, ring, 1, 1)))
    absolute = place(np.arange(dp).reshape(1, dp, 1, 1), np.arange(ring).reshape(ring, 1, 1, 1))
    return np.stack(table).astype(np.int32), absolute.reshape(-1, 1).astype(np.int32)


def view_rows(*sizes):
    return row_tables(*sizes)[1]


def body(sizes, level_in, out_grad, view_qkv, view_out, time_qkv, time_out):
    z, xl, core, dp = sizes
    frames = z * xl * core
    entries = float(dp * 2 * PX * CH)
    frame_axes = ("z", "xl", "core")
    mates = ("view", "dp")
    group = 2 * dp
    spot = (lax.axis_index("view") * xl + lax.axis_index("xl")) * dp + lax.axis_index("dp")
    place = jnp.stack([lax.axis_index("view"), lax.axis_index("core"), spot]).astype(jnp.int32)
    table = jnp.asarray(row_tables(z, xl, core, dp)[0])
    rows = D // (z * xl * core * dp)
    stats = ((group, 2 * VIEWS, 128), F32)
    tok32, tok16 = ((T, D), F32), ((T, D), BF16)
    half32, half16 = ((HALF, D), F32), ((HALF, D), BF16)
    wide = ((T, 4 * D), BF16)
    moved = ((frames, T // frames, 2 * D), BF16)

    def share(field):
        return lax.all_to_all(field, mates, 0, 0, tiled=True)

    def transpose(field):
        return lax.all_to_all(field, frame_axes, 0, 0, tiled=True)

    def swap(field, axis):
        return lax.ppermute(field, axis, [(0, 1), (1, 0)])

    def shifted(pieces, axis):
        return [
            lax.ppermute(piece, axis, [(i, (i + step + 1) % 4) for i in range(4)]) for step, piece in enumerate(pieces)
        ]

    def crossed(field, step):
        return field + lax.ppermute(field, "dp", [(i, i ^ step) for i in range(dp)])

    views = VIEWS // 2
    rows16 = ((2 * VIEWS, 128), F32)
    x_other, og_other = swap(level_in, "view"), swap(out_grad, "view")
    (st1,) = call(k_first_stats, [stats], level_in, place=place)
    stream, packed_one, sides, own, st2 = call(
        functools.partial(k_view, entries), [tok32, ((T, 3 * D), BF16), ((T, 2 * D), BF16), rows16, stats],
        level_in, x_other, share(st1), view_qkv, view_out, place=place, us=4,
    )
    column = jnp.asarray(view_rows(z, xl, core, dp))
    (left,) = call(k_left_sides, [((2, D, 2 * T), BF16)], column, sides, swap(sides, "core"), place=place)
    out_field, rows_two = call(
        functools.partial(k_norm_two, entries), [moved, rows16], stream, out_grad, og_other, share(st2), place=place
    )
    back, keep_two, give_two = call(k_time, [moved, wide, wide], transpose(out_field), time_qkv, time_out, place=place, us=6)
    mine, *pieces = call(
        k_weights_time, [((D // 4, 2 * D), BF16)] * 4, table, keep_two, swap(give_two, "core"), place=place, us=3
    )
    moved_back, _, left = lax.optimization_barrier((transpose(back), pieces, left))
    time_parts = [mine, *shifted(pieces, "dp")]
    (st3,) = call(k_back_stats, [stats], moved_back, stream, rows_two, us=1)
    shared, time_parts = lax.optimization_barrier((share(st3), time_parts))
    keep_one, give_one, pgrad, stream_grad, sums_two = call(
        functools.partial(k_view_back, entries), [((T, 2 * D), BF16)] * 2 + [((T, 3 * D), BF16), tok32, rows16],
        moved_back, stream, rows_two, shared, out_grad, og_other, packed_one, view_out, place=place, us=5,
    )
    (partial,) = call(k_weights_view, [((D, 2 * D), BF16)], left, keep_one, swap(give_one, "core"), us=1)
    time_parts, partial, pgrad = lax.optimization_barrier((time_parts, partial, pgrad))
    u_keep, o_keep, send_back, st4 = call(
        k_view_stats, [half32, half16, ((HALF, 2 * D), BF16), rows16],
        pgrad, stream_grad, moved_back, stream, level_in, x_other, own, view_qkv, place=place, us=3,
    )
    parts = lax.all_to_all(partial, ("view", "xl", "dp"), 0, 0, tiled=True)
    mine, *pieces = call(k_sum_time, [((D // 16, 2 * D), BF16)] * 4, *time_parts)
    time_parts = [mine, *shifted(pieces, ("view", "xl"))]
    parts, time_parts, st4 = lax.optimization_barrier((parts, time_parts, crossed(crossed(st4, 2), 1)))
    (by_z,) = call(k_sum_rows, [((z, 4, rows * D), BF16)], parts, *time_parts)
    by_z, st4, send_back = lax.optimization_barrier((by_z, st4, send_back))
    by_z = lax.all_to_all(by_z, "z", 0, 0, tiled=True)
    recv_back = swap(send_back, "view")
    st4 = st4 + swap(st4, "view")
    by_z, st4, recv_back = lax.optimization_barrier((by_z, st4, recv_back))
    (summed,) = call(k_sum, [((4, rows * D), BF16)], by_z)
    level_out, level_in_grad, sums = call(
        functools.partial(k_finish, entries),
        [((views, 2 * PX, D), BF16), ((views, 2 * PX, D), BF16), ((4, views, 128), F32)],
        st4, sums_two, own, level_in, u_keep, o_keep, recv_back, place=place, us=3,
    )
    first = place[1] == 0
    near = swap(summed, "core")
    pair = jnp.concatenate([jnp.where(first, summed, near), jnp.where(first, near, summed)], axis=0)
    qkv_row, out_row = ((rows, 3 * D), BF16), ((rows, D), BF16)
    view_qkv_grad, view_out_grad, time_qkv_grad, time_out_grad = call(
        k_rows, [qkv_row, out_row, qkv_row, out_row], pair, swap(pair, "view"), place=place
    )
    return (
        level_out.reshape(level_in.shape),
        level_in_grad.reshape(level_in.shape),
        view_qkv_grad,
        view_out_grad,
        time_qkv_grad,
        time_out_grad,
        sums[:, :, :GROUPS].reshape(2, 2, views, 1, GROUPS),
    )


def solution(mesh):
    frames, dp = mesh.shape["frame"], mesh.shape["dp"]
    sizes = (frames // 4, 2, 2, dp)
    fine = Mesh(mesh.devices.reshape((2,) + sizes), ("view", "z", "xl", "core", "dp"))
    split = ("z", "xl", "core")
    tokens = P("view", split, "dp", None)
    rows = P(split + ("dp",), None)
    return jax.shard_map(
        functools.partial(body, sizes),
        mesh=fine,
        in_specs=(tokens, tokens, P(), P(), P(), P()),
        out_specs=(tokens, tokens, rows, rows, rows, rows, P(None, None, "view", split, None)),
        check_vma=False,
    )
```

```python
import functools

import jax
import jax.numpy as jnp
import numpy as np
from jax import lax
from jax.experimental import pallas as pl
from jax.experimental.pallas import tpu as pltpu
from jax.sharding import Mesh, PartitionSpec as P

HEADS = 10
HD = 64
GROUPS = 32
EPS = 1e-05
D = 640
CH = D // GROUPS
VIEWS = 8
PX = 16
T = VIEWS * PX
HALF = T // 2
SCALE = HD ** (-0.5)
F32 = jnp.float32
BF16 = jnp.bfloat16
VMEM_LIMIT = 32


def group_matrix():
    row = lax.broadcasted_iota(jnp.int32, (D, 128), 0)
    low = lax.broadcasted_iota(jnp.int32, (D, 128), 1) * CH
    return ((row >= low) & (row < low + CH)).astype(F32).astype(BF16)


def three_parts(rows):
    high = rows.astype(BF16)
    rest = rows - high.astype(F32)
    middle = rest.astype(BF16)
    return high, middle, (rest - middle.astype(F32)).astype(BF16)


def exact_product(rows, member, dims):
    count = rows.shape[0]
    stacked = jnp.concatenate([part.astype(F32) for part in three_parts(rows)], axis=0).astype(BF16)
    out = lax.dot_general(stacked, member, (dims, ((), ())), preferred_element_type=F32)
    return out[:count] + (out[count : 2 * count] + out[2 * count :])


def to_groups(rows, member):
    return exact_product(rows, member, ((1,), (0,)))


def to_channels(groups, member):
    return exact_product(groups, member, ((1,), (1,)))


def both_sums(grad, normed, member):
    return to_groups(jnp.concatenate([view_sum(grad), view_sum(grad * normed)], axis=0), member)


def view_sum(tokens):
    return jnp.sum(tokens.reshape(tokens.shape[0] // PX, PX, D), axis=1)


def per_token(rows):
    return jnp.broadcast_to(rows[:, None, :], (rows.shape[0], PX, D)).reshape(rows.shape[0] * PX, D)


def partial_stats(tokens, member):
    mean = to_groups(view_sum(tokens), member) * (1.0 / (PX * CH))
    centred = tokens - per_token(to_channels(mean, member))
    return jnp.concatenate([mean, to_groups(view_sum(centred * centred), member)], axis=0)


def merge_stats(means, spreads, entries):
    count = len(means)
    mean = sum(means) * (1.0 / count)
    spread = sum(spreads)
    for other in means:
        gap = other - mean
        spread = spread + gap * gap * float(PX * CH)
    return mean, lax.rsqrt(spread * (1.0 / entries) + EPS)


def spread_out(ref, both):
    ref[...] = jnp.broadcast_to(both[None], ref.shape)


def mm(left, right):
    return jnp.dot(left, right, preferred_element_type=F32)


def mm_t(left, right):
    return lax.dot_general(left, right, (((1,), (1,)), ((), ())), preferred_element_type=F32)


def t_mm(left, right):
    return lax.dot_general(left, right, (((0,), (0,)), ((), ())), preferred_element_type=F32)


def lane_low(rows):
    return lax.broadcasted_iota(jnp.int32, (rows, 128), 1) < HD


def both_heads(pair):
    low = lane_low(pair.shape[0])
    zero = jnp.zeros_like(pair)
    return jnp.concatenate([jnp.where(low, pair, zero), jnp.where(low, zero, pair)], axis=0)


def join_heads(stacked):
    return jnp.where(lane_low(T), stacked[:T], stacked[T:])


def same_sequence(period):
    row = lax.broadcasted_iota(jnp.int32, (2 * T, T), 0)
    col = lax.broadcasted_iota(jnp.int32, (2 * T, T), 1)
    return ((row ^ col) & (period - 1)) == 0


def softmax_all(stacked_q, keys, allowed):
    scores = jnp.concatenate([mm_t(q, k) for q, k in zip(stacked_q, keys)], axis=0)
    allowed = jnp.concatenate([allowed] * len(keys), axis=0)
    scores = jnp.where(allowed, scores * SCALE, -1e30)
    top = jnp.max(scores, axis=-1, keepdims=True)
    weights = jnp.exp(scores - top)
    return weights * (1.0 / jnp.sum(weights, axis=-1, keepdims=True))


def pair_of(index):
    return slice(index * 128, (index + 1) * 128)


def pieces_of(packed, first):
    return [packed[:, pair_of(first + pair)] for pair in range(HEADS // 2)]


def rows_of(stacked, pair):
    return stacked[pair * 2 * T : (pair + 1) * 2 * T]


def attend(packed, allowed):
    q, k, v = [both_heads(piece) for piece in pieces_of(packed, 0)], pieces_of(packed, 5), pieces_of(packed, 10)
    prob = softmax_all(q, k, allowed)
    rounded = prob.astype(BF16)
    outs = [join_heads(mm(rows_of(rounded, pair), v[pair])).astype(BF16) for pair in range(HEADS // 2)]
    return jnp.concatenate(outs, axis=1), prob


def attend_back(grad, packed, allowed, prob=None):
    q, k, v = [both_heads(piece) for piece in pieces_of(packed, 0)], pieces_of(packed, 5), pieces_of(packed, 10)
    g = [both_heads(piece) for piece in pieces_of(grad, 0)]
    if prob is None:
        prob = softmax_all(q, k, allowed)
    rounded = prob.astype(BF16)
    dprob = jnp.concatenate([mm_t(x, y) for x, y in zip(g, v)], axis=0)
    dscore = prob * (dprob - jnp.sum(dprob * prob, axis=-1, keepdims=True))
    dscore = (dscore * SCALE).astype(BF16)
    pairs = range(HEADS // 2)
    dvs = [t_mm(rows_of(rounded, pair), g[pair]).astype(BF16) for pair in pairs]
    dqs = [join_heads(mm(rows_of(dscore, pair), k[pair])).astype(BF16) for pair in pairs]
    dks = [t_mm(rows_of(dscore, pair), q[pair]).astype(BF16) for pair in pairs]
    return jnp.concatenate(dqs + dks + dvs, axis=1)


def halves(ref, first):
    low = ref[:, 0, 0:PX, :].reshape(HALF, D)
    high = ref[:, 0, PX : 2 * PX, :].reshape(HALF, D)
    return jnp.where(first, low, high), jnp.where(first, high, low)


def regrouped(own_ref, other_ref, first):
    mine, theirs = halves(own_ref, first)[0], halves(other_ref, first)[0]
    return jnp.concatenate([jnp.where(first, mine, theirs), jnp.where(first, theirs, mine)], axis=0)


def k_first_stats(x_ref, stats_ref):
    low, high = x_ref[:, 0, 0:PX, :].reshape(HALF, D), x_ref[:, 0, PX : 2 * PX, :].reshape(HALF, D)
    tokens = jnp.concatenate([low, high], axis=0).astype(F32)
    spread_out(stats_ref, partial_stats(tokens, group_matrix()))


def normalized(x, rows, member):
    channels = to_channels(rows, member)
    return (x - per_token(channels[:VIEWS])) * per_token(channels[VIEWS:])


def k_view(entries, place, x_ref, other_ref, g_ref, wqkv_ref, wout_ref, stream_ref, saved_ref, sides_ref, own_ref, stats_ref):
    first = place[0] == 0
    member = group_matrix()
    sources = g_ref.shape[0]
    half = VIEWS // 2

    def side(low):
        chosen = range(low, low + sources // 2)
        means = [g_ref[s, a * half : (a + 1) * half, :] for s in chosen for a in range(2)]
        spreads = [g_ref[s, VIEWS + a * half : VIEWS + (a + 1) * half, :] for s in chosen for a in range(2)]
        return merge_stats(means, spreads, entries)

    low, high = side(0), side(sources // 2)
    rows = jnp.concatenate([low[0], high[0], low[1], high[1]], axis=0)
    own_ref[...] = rows
    x = regrouped(x_ref, other_ref, first).astype(F32)
    hidden = normalized(x, rows, member).astype(BF16)
    packed = mm(hidden, wqkv_ref[...]).astype(BF16)
    saved_ref[...] = packed
    mixed, _ = attend(packed, same_sequence(PX))
    sides_ref[:, :D] = hidden
    sides_ref[:, D:] = mixed
    stream = x + mm(mixed, wout_ref[...])
    stream_ref[...] = stream
    spread_out(stats_ref, partial_stats(stream, member))


def k_norm_two(entries, place, stream_ref, grad_ref, other_ref, g_ref, send_ref, rows_ref):
    member = group_matrix()
    sources = range(g_ref.shape[0])
    mean, inverse = merge_stats(
        [g_ref[s, 0:VIEWS, :] for s in sources], [g_ref[s, VIEWS:, :] for s in sources], entries
    )
    rows = jnp.concatenate([mean, inverse], axis=0)
    rows_ref[...] = rows
    shape = send_ref.shape[:2] + (D,)
    send_ref[:, :, :D] = normalized(stream_ref[...], rows, member).astype(BF16).reshape(shape)
    send_ref[:, :, D:] = regrouped(grad_ref, other_ref, place[0] == 0).reshape(shape)


def weight_sides(core, hidden, mixed, packed_grad, grad, keep_ref, give_ref):
    first = core == 0
    keep_ref[:, :D] = hidden
    give_ref[:, :D] = hidden
    keep_ref[:, D : 2 * D] = jnp.where(first, hidden, mixed)
    give_ref[:, D : 2 * D] = jnp.where(first, mixed, hidden)
    right_sides(core, packed_grad, grad, keep_ref, give_ref, 2 * D)


def right_sides(core, packed_grad, grad, keep_ref, give_ref, start=0):
    first = core == 0
    quarter = packed_grad[:, :D], packed_grad[:, D : 2 * D], packed_grad[:, 2 * D :], grad
    for slot in range(2):
        cols = slice(start + slot * D, start + (slot + 1) * D)
        keep_ref[:, cols] = jnp.where(first, quarter[slot], quarter[2 + slot])
        give_ref[:, cols] = jnp.where(first, quarter[2 + slot], quarter[slot])


def k_time(place, recv_ref, wqkv_ref, wout_ref, back_ref, keep_ref, give_ref):
    hidden = recv_ref[:, :, :D].reshape(T, D)
    grad = recv_ref[:, :, D:].reshape(T, D)
    allowed = same_sequence(recv_ref.shape[1])
    packed = mm(hidden, wqkv_ref[...]).astype(BF16)
    mixed, probs = attend(packed, allowed)
    shape = back_ref.shape[:2] + (D,)
    back_ref[:, :, :D] = mm(mixed, wout_ref[...]).astype(BF16).reshape(shape)
    packed_grad = attend_back(mm_t(grad, wout_ref[...]).astype(BF16), packed, allowed, probs)
    back_ref[:, :, D:] = mm_t(packed_grad, wqkv_ref[...]).astype(BF16).reshape(shape)
    weight_sides(place[1], hidden, mixed, packed_grad, grad, keep_ref, give_ref)


def k_back_stats(back_ref, stream_ref, rows_ref, stats_ref):
    member = group_matrix()
    grad = back_ref[:, :, D:].reshape(T, D).astype(F32)
    spread_out(stats_ref, both_sums(grad, normalized(stream_ref[...], rows_ref[...], member), member))


def k_view_back(entries, place, back_ref, stream_ref, rows_ref, g_ref, og_ref, ogother_ref, packed_ref, wout_ref,
                keep_ref, give_ref, pgrad_ref, stream_grad_ref, sums_ref):
    first = place[0] == 0
    member = group_matrix()
    sums = g_ref[0]
    for s in range(1, g_ref.shape[0]):
        sums = sums + g_ref[s]
    sums_ref[...] = sums
    channels = to_channels(jnp.concatenate([sums * (1.0 / entries), rows_ref[...]], axis=0), member)
    m1, m2, mean, inverse = (per_token(channels[k * VIEWS : (k + 1) * VIEWS]) for k in range(4))
    normed_two = (stream_ref[...] - mean) * inverse
    ghid = back_ref[:, :, D:].reshape(T, D).astype(F32)
    grad_stream = regrouped(og_ref, ogother_ref, first).astype(F32) + inverse * (ghid - m1 - normed_two * m2)
    stream_grad_ref[...] = grad_stream
    grad_b = grad_stream.astype(BF16)
    packed_grad = attend_back(mm_t(grad_b, wout_ref[...]).astype(BF16), packed_ref[...], same_sequence(PX))
    pgrad_ref[...] = packed_grad
    right_sides(place[1], packed_grad, grad_b, keep_ref, give_ref)


def k_view_stats(place, pgrad_ref, stream_grad_ref, back_ref, stream_ref, x_ref, other_ref, own_ref, wqkv_ref,
                 ukeep_ref, okeep_ref, send_ref, stats_ref):
    first = place[0] == 0
    member = group_matrix()
    grad = mm_t(pgrad_ref[...], wqkv_ref[...]).astype(BF16).astype(F32)
    channels = to_channels(own_ref[...], member)
    mean, inverse = per_token(channels[:VIEWS]), per_token(channels[VIEWS:])
    normed = (regrouped(x_ref, other_ref, first).astype(F32) - mean) * inverse
    stats_ref[...] = both_sums(grad, normed, member)
    partly = stream_grad_ref[...] + inverse * grad
    temporal = back_ref[:, :, :D].reshape(T, D).astype(F32)
    out = (stream_ref[...] + temporal).astype(BF16)
    ukeep_ref[...] = jnp.where(first, partly[:HALF], partly[HALF:])
    okeep_ref[...] = jnp.where(first, out[:HALF], out[HALF:])
    send_ref[:, :D] = jnp.where(first, partly[HALF:], partly[:HALF]).astype(BF16)
    send_ref[:, D:] = jnp.where(first, out[HALF:], out[:HALF])


def k_finish(entries, place, g_ref, sumstwo_ref, own_ref, x_ref, ukeep_ref, okeep_ref, recv_ref,
             out_ref, grad_ref, sums_ref):
    first = place[0] == 0
    member = group_matrix()
    half = VIEWS // 2
    sums = g_ref[...]

    def mine(rows):
        return jnp.where(first, rows[:half], rows[half:])

    s1, s2 = mine(sums[:VIEWS]), mine(sums[VIEWS:])
    sums_ref[0] = s1
    sums_ref[1] = s2
    sums_ref[2] = mine(sumstwo_ref[0:VIEWS, :])
    sums_ref[3] = mine(sumstwo_ref[VIEWS:, :])
    inverse = mine(own_ref[VIEWS:, :])
    scale = inverse * (1.0 / entries)
    rows = jnp.concatenate([mine(own_ref[0:VIEWS, :]), inverse, s1 * scale, s2 * scale], axis=0)
    channels = to_channels(rows, member)
    mean_c, inverse_c, a, b = (per_token(channels[k * half : (k + 1) * half]) for k in range(4))

    def finished(part, x):
        normed = (x.astype(F32) - mean_c) * inverse_c
        return (part.astype(F32) - a - normed * b).astype(BF16)

    x_keep, x_give = halves(x_ref, first)
    keep = finished(ukeep_ref[...], x_keep)
    other = finished(recv_ref[:, :D], x_give)
    shape = (half, PX, D)
    grad_ref[:, 0:PX, :] = jnp.where(first, keep, other).reshape(shape)
    grad_ref[:, PX:, :] = jnp.where(first, other, keep).reshape(shape)
    okeep, orecv = okeep_ref[...], recv_ref[:, D:]
    out_ref[:, 0:PX, :] = jnp.where(first, okeep, orecv).reshape(shape)
    out_ref[:, PX:, :] = jnp.where(first, orecv, okeep).reshape(shape)


def added32(*refs):
    total = refs[0][...].astype(F32)
    for ref in refs[1:]:
        total = total + ref[...].astype(F32)
    return total


def added(*refs):
    return added32(*refs).astype(BF16)


def split_rows(total, refs, cols=slice(None)):
    rows = total.shape[0] // len(refs)
    for s, ref in enumerate(refs):
        ref[:, cols] = total[s * rows : (s + 1) * rows].astype(BF16)


def weight_tile(unit, order, keep_ref, recv_ref):
    left = jnp.concatenate([keep_ref[:, unit * D : (unit + 1) * D], recv_ref[:, unit * D : (unit + 1) * D]], axis=0)
    cols = slice((2 + unit) * D, (3 + unit) * D)
    right = jnp.concatenate([keep_ref[:, cols], recv_ref[:, cols]], axis=0)
    return t_mm(mm(left, order).astype(BF16), right)


def k_weights_time(place, table_ref, keep_ref, recv_ref, *out_refs):
    order = (lax.broadcasted_iota(jnp.int32, (D, D), 0) == table_ref[place[2]]).astype(BF16)
    for unit in range(2):
        total = weight_tile(unit, order, keep_ref, recv_ref)
        split_rows(total, out_refs, slice(unit * D, (unit + 1) * D))


def k_left_sides(place, column_ref, mine_ref, theirs_ref, left_ref):
    first = place[1] == 0
    order = (lax.broadcasted_iota(jnp.int32, (D, D), 1) == column_ref[...]).astype(BF16)
    hidden = jnp.concatenate([mine_ref[:, :D], theirs_ref[:, :D]], axis=0)
    mixed = jnp.concatenate([mine_ref[:, D:], theirs_ref[:, D:]], axis=0)
    left_ref[0] = mm_t(order, hidden).astype(BF16)
    left_ref[1] = mm_t(order, jnp.where(first, hidden, mixed)).astype(BF16)


def k_weights_view(left_ref, mine_ref, theirs_ref, out_ref):
    for unit in range(2):
        cols = slice(unit * D, (unit + 1) * D)
        right = jnp.concatenate([mine_ref[:, cols], theirs_ref[:, cols]], axis=0)
        out_ref[:, cols] = mm(left_ref[unit], right).astype(BF16)


def k_sum_time(*refs):
    split_rows(added32(*refs[:4]), refs[4:])


def k_sum_rows(parts_ref, *refs):
    times, out_ref = refs[:4], refs[4]
    chips = out_ref.shape[0]
    rows = times[0].shape[0]
    count = parts_ref.shape[0] // rows
    parts = parts_ref[...].astype(F32)
    view = sum(parts[s * rows : (s + 1) * rows] for s in range(count))
    time = added32(*times)
    units = [view[:, :D], view[:, D:], time[:, :D], time[:, D:]]
    for row in range(out_ref.shape[2] // D):
        block = jnp.stack([unit[row * chips : (row + 1) * chips] for unit in units], axis=1)
        out_ref[:, :, row * D : (row + 1) * D] = block.astype(BF16)


def k_sum(parts_ref, out_ref):
    total = parts_ref[0].astype(F32)
    for s in range(1, parts_ref.shape[0]):
        total = total + parts_ref[s].astype(F32)
    out_ref[...] = total.astype(BF16)


def k_rows(place, near_ref, far_ref, vqkv_ref, vout_ref, tqkv_ref, tout_ref):
    both = jnp.where(place[0] == place[1], near_ref[...].astype(F32), far_ref[...].astype(F32))
    rows = vout_ref.shape[0]

    def lines(unit):
        return jnp.concatenate([both[unit : unit + 1, row * D : (row + 1) * D] for row in range(rows)], axis=0)

    for unit, qkv_ref, out_ref in ((0, vqkv_ref, vout_ref), (2, tqkv_ref, tout_ref)):
        qkv_ref[...] = jnp.concatenate([lines(unit), lines(unit + 1), lines(unit + 4)], axis=1).astype(BF16)
        out_ref[...] = lines(unit + 5).astype(BF16)


def call(kernel, outs, *args, place=None, us=2, vmem=VMEM_LIMIT):
    specs = [pl.BlockSpec(memory_space=pltpu.VMEM)] * len(args)
    if place is not None:
        specs = [pl.BlockSpec(memory_space=pltpu.SMEM)] + specs
        args = (place,) + args
    return pl.pallas_call(
        kernel,
        out_shape=[jax.ShapeDtypeStruct(shape, dtype) for shape, dtype in outs],
        in_specs=specs,
        out_specs=[pl.BlockSpec(memory_space=pltpu.VMEM)] * len(outs),
        compiler_params=pltpu.CompilerParams(vmem_limit_bytes=vmem * 1024 * 1024),
        cost_estimate=pl.CostEstimate(flops=int(us * 1e9), bytes_accessed=int(us * 3e6), transcendentals=0),
    )(*args)


def row_tables(z, xl, core, dp):
    rows = D // (z * xl * core * dp)
    ring = core * xl
    chip = np.arange(z).reshape(1, 1, 1, z)
    row = np.arange(rows).reshape(1, 1, rows, 1)

    def place(y, x):
        return ((((chip * xl + x % xl) * core + x // xl) * dp + y) * rows + row).reshape(1, -1)

    table = []
    for me_x in range(ring):
        for me_dp in range(dp):
            y, x = (me_dp + np.arange(dp)) % dp, (me_x + np.arange(ring)) % ring
            table.append(place(y.reshape(dp, 1, 1, 1), x.reshape(1, ring, 1, 1)))
    absolute = place(np.arange(dp).reshape(1, dp, 1, 1), np.arange(ring).reshape(ring, 1, 1, 1))
    return np.stack(table).astype(np.int32), absolute.reshape(-1, 1).astype(np.int32)


def view_rows(*sizes):
    return row_tables(*sizes)[1]


def body(sizes, level_in, out_grad, view_qkv, view_out, time_qkv, time_out):
    z, xl, core, dp = sizes
    frames = z * xl * core
    entries = float(dp * 2 * PX * CH)
    frame_axes = ("z", "xl", "core")
    mates = ("view", "dp")
    group = 2 * dp
    spot = (lax.axis_index("view") * xl + lax.axis_index("xl")) * dp + lax.axis_index("dp")
    place = jnp.stack([lax.axis_index("view"), lax.axis_index("core"), spot]).astype(jnp.int32)
    table = jnp.asarray(row_tables(z, xl, core, dp)[0])
    rows = D // (z * xl * core * dp)
    stats = ((group, 2 * VIEWS, 128), F32)
    tok32, tok16 = ((T, D), F32), ((T, D), BF16)
    half32, half16 = ((HALF, D), F32), ((HALF, D), BF16)
    wide = ((T, 4 * D), BF16)
    moved = ((frames, T // frames, 2 * D), BF16)

    def share(field):
        return lax.all_to_all(field, mates, 0, 0, tiled=True)

    def transpose(field):
        return lax.all_to_all(field, frame_axes, 0, 0, tiled=True)

    def swap(field, axis):
        return lax.ppermute(field, axis, [(0, 1), (1, 0)])

    def shifted(pieces, axis):
        return [
            lax.ppermute(piece, axis, [(i, (i + step + 1) % 4) for i in range(4)]) for step, piece in enumerate(pieces)
        ]

    def crossed(field, step):
        return field + lax.ppermute(field, "dp", [(i, i ^ step) for i in range(dp)])

    views = VIEWS // 2
    rows16 = ((2 * VIEWS, 128), F32)
    x_other, og_other = swap(level_in, "view"), swap(out_grad, "view")
    (st1,) = call(k_first_stats, [stats], level_in)
    stream, packed_one, sides, own, st2 = call(
        functools.partial(k_view, entries), [tok32, ((T, 3 * D), BF16), ((T, 2 * D), BF16), rows16, stats],
        level_in, x_other, share(st1), view_qkv, view_out, place=place, us=4,
    )
    column = jnp.asarray(view_rows(z, xl, core, dp))
    (left,) = call(k_left_sides, [((2, D, 2 * T), BF16)], column, sides, swap(sides, "core"), place=place)
    out_field, rows_two = call(
        functools.partial(k_norm_two, entries), [moved, rows16], stream, out_grad, og_other, share(st2), place=place
    )
    back, keep_two, give_two = call(k_time, [moved, wide, wide], transpose(out_field), time_qkv, time_out, place=place, us=6)
    mine, *pieces = call(
        k_weights_time, [((D // 4, 2 * D), BF16)] * 4, table, keep_two, swap(give_two, "core"), place=place, us=3
    )
    moved_back, _, left = lax.optimization_barrier((transpose(back), pieces, left))
    time_parts = [mine, *shifted(pieces, "dp")]
    (st3,) = call(k_back_stats, [stats], moved_back, stream, rows_two, us=1)
    shared, time_parts = lax.optimization_barrier((share(st3), time_parts))
    keep_one, give_one, pgrad, stream_grad, sums_two = call(
        functools.partial(k_view_back, entries), [((T, 2 * D), BF16)] * 2 + [((T, 3 * D), BF16), tok32, rows16],
        moved_back, stream, rows_two, shared, out_grad, og_other, packed_one, view_out, place=place, us=5,
    )
    (partial,) = call(k_weights_view, [((D, 2 * D), BF16)], left, keep_one, swap(give_one, "core"), us=1)
    time_parts, partial, pgrad = lax.optimization_barrier((time_parts, partial, pgrad))
    u_keep, o_keep, send_back, st4 = call(
        k_view_stats, [half32, half16, ((HALF, 2 * D), BF16), rows16],
        pgrad, stream_grad, moved_back, stream, level_in, x_other, own, view_qkv, place=place, us=3,
    )
    parts = lax.all_to_all(partial, ("view", "xl", "dp"), 0, 0, tiled=True)
    mine, *pieces = call(k_sum_time, [((D // 16, 2 * D), BF16)] * 4, *time_parts)
    time_parts = [mine, *shifted(pieces, ("view", "xl"))]
    parts, time_parts, st4 = lax.optimization_barrier((parts, time_parts, crossed(crossed(st4, 2), 1)))
    (by_z,) = call(k_sum_rows, [((z, 4, rows * D), BF16)], parts, *time_parts)
    by_z, st4, send_back = lax.optimization_barrier((by_z, st4, send_back))
    by_z = lax.all_to_all(by_z, "z", 0, 0, tiled=True)
    recv_back = swap(send_back, "view")
    st4 = st4 + swap(st4, "view")
    by_z, st4, recv_back = lax.optimization_barrier((by_z, st4, recv_back))
    (summed,) = call(k_sum, [((4, rows * D), BF16)], by_z)
    level_out, level_in_grad, sums = call(
        functools.partial(k_finish, entries),
        [((views, 2 * PX, D), BF16), ((views, 2 * PX, D), BF16), ((4, views, 128), F32)],
        st4, sums_two, own, level_in, u_keep, o_keep, recv_back, place=place, us=3,
    )
    first = place[1] == 0
    near = swap(summed, "core")
    pair = jnp.concatenate([jnp.where(first, summed, near), jnp.where(first, near, summed)], axis=0)
    qkv_row, out_row = ((rows, 3 * D), BF16), ((rows, D), BF16)
    view_qkv_grad, view_out_grad, time_qkv_grad, time_out_grad = call(
        k_rows, [qkv_row, out_row, qkv_row, out_row], pair, swap(pair, "view"), place=place
    )
    return (
        level_out.reshape(level_in.shape),
        level_in_grad.reshape(level_in.shape),
        view_qkv_grad,
        view_out_grad,
        time_qkv_grad,
        time_out_grad,
        sums[:, :, :GROUPS].reshape(2, 2, views, 1, GROUPS),
    )


def solution(mesh):
    frames, dp = mesh.shape["frame"], mesh.shape["dp"]
    sizes = (frames // 4, 2, 2, dp)
    fine = Mesh(mesh.devices.reshape((2,) + sizes), ("view", "z", "xl", "core", "dp"))
    split = ("z", "xl", "core")
    tokens = P("view", split, "dp", None)
    rows = P(split + ("dp",), None)
    return jax.shard_map(
        functools.partial(body, sizes),
        mesh=fine,
        in_specs=(tokens, tokens, P(), P(), P(), P()),
        out_specs=(tokens, tokens, rows, rows, rows, rows, P(None, None, "view", split, None)),
        check_vma=False,
    )
```

```python
import functools

import jax
import jax.numpy as jnp
import numpy as np
from jax import lax
from jax.experimental import pallas as pl
from jax.experimental.pallas import tpu as pltpu
from jax.sharding import Mesh, PartitionSpec as P

HEADS = 10
HD = 64
GROUPS = 32
EPS = 1e-05
D = 640
CH = D // GROUPS
VIEWS = 8
PX = 16
T = VIEWS * PX
HALF = T // 2
SCALE = HD ** (-0.5)
F32 = jnp.float32
BF16 = jnp.bfloat16
VMEM_LIMIT = 32


def group_matrix():
    row = lax.broadcasted_iota(jnp.int32, (D, 128), 0)
    low = lax.broadcasted_iota(jnp.int32, (D, 128), 1) * CH
    return ((row >= low) & (row < low + CH)).astype(F32).astype(BF16)


def three_parts(rows):
    high = rows.astype(BF16)
    rest = rows - high.astype(F32)
    middle = rest.astype(BF16)
    return high, middle, (rest - middle.astype(F32)).astype(BF16)


def exact_product(rows, member, dims):
    count = rows.shape[0]
    stacked = jnp.concatenate([part.astype(F32) for part in three_parts(rows)], axis=0).astype(BF16)
    out = lax.dot_general(stacked, member, (dims, ((), ())), preferred_element_type=F32)
    return out[:count] + (out[count : 2 * count] + out[2 * count :])


def to_groups(rows, member):
    return exact_product(rows, member, ((1,), (0,)))


def to_channels(groups, member):
    return exact_product(groups, member, ((1,), (1,)))


def both_sums(grad, normed, member):
    return to_groups(jnp.concatenate([view_sum(grad), view_sum(grad * normed)], axis=0), member)


def view_sum(tokens):
    return jnp.sum(tokens.reshape(tokens.shape[0] // PX, PX, D), axis=1)


def per_token(rows):
    return jnp.broadcast_to(rows[:, None, :], (rows.shape[0], PX, D)).reshape(rows.shape[0] * PX, D)


def partial_stats(tokens, member):
    mean = to_groups(view_sum(tokens), member) * (1.0 / (PX * CH))
    centred = tokens - per_token(to_channels(mean, member))
    return jnp.concatenate([mean, to_groups(view_sum(centred * centred), member)], axis=0)


def merge_stats(means, spreads, entries):
    count = len(means)
    mean = sum(means) * (1.0 / count)
    spread = sum(spreads)
    for other in means:
        gap = other - mean
        spread = spread + gap * gap * float(PX * CH)
    return mean, lax.rsqrt(spread * (1.0 / entries) + EPS)


def spread_out(ref, both):
    ref[...] = jnp.broadcast_to(both[None], ref.shape)


def mm(left, right):
    return jnp.dot(left, right, preferred_element_type=F32)


def mm_t(left, right):
    return lax.dot_general(left, right, (((1,), (1,)), ((), ())), preferred_element_type=F32)


def t_mm(left, right):
    return lax.dot_general(left, right, (((0,), (0,)), ((), ())), preferred_element_type=F32)


def lane_low(rows):
    return lax.broadcasted_iota(jnp.int32, (rows, 128), 1) < HD


def both_heads(pair):
    low = lane_low(pair.shape[0])
    zero = jnp.zeros_like(pair)
    return jnp.concatenate([jnp.where(low, pair, zero), jnp.where(low, zero, pair)], axis=0)


def join_heads(stacked):
    return jnp.where(lane_low(T), stacked[:T], stacked[T:])


def same_sequence(period):
    row = lax.broadcasted_iota(jnp.int32, (2 * T, T), 0)
    col = lax.broadcasted_iota(jnp.int32, (2 * T, T), 1)
    return ((row ^ col) & (period - 1)) == 0


def softmax_all(stacked_q, keys, allowed):
    scores = jnp.concatenate([mm_t(q, k) for q, k in zip(stacked_q, keys)], axis=0)
    allowed = jnp.concatenate([allowed] * len(keys), axis=0)
    scores = jnp.where(allowed, scores * SCALE, -1e30)
    top = jnp.max(scores, axis=-1, keepdims=True)
    weights = jnp.exp(scores - top)
    return weights * (1.0 / jnp.sum(weights, axis=-1, keepdims=True))


def pair_of(index):
    return slice(index * 128, (index + 1) * 128)


def pieces_of(packed, first):
    return [packed[:, pair_of(first + pair)] for pair in range(HEADS // 2)]


def rows_of(stacked, pair):
    return stacked[pair * 2 * T : (pair + 1) * 2 * T]


def attend(packed, allowed):
    q, k, v = [both_heads(piece) for piece in pieces_of(packed, 0)], pieces_of(packed, 5), pieces_of(packed, 10)
    prob = softmax_all(q, k, allowed)
    rounded = prob.astype(BF16)
    outs = [join_heads(mm(rows_of(rounded, pair), v[pair])).astype(BF16) for pair in range(HEADS // 2)]
    return jnp.concatenate(outs, axis=1), prob


def attend_back(grad, packed, allowed, prob=None):
    q, k, v = [both_heads(piece) for piece in pieces_of(packed, 0)], pieces_of(packed, 5), pieces_of(packed, 10)
    g = [both_heads(piece) for piece in pieces_of(grad, 0)]
    if prob is None:
        prob = softmax_all(q, k, allowed)
    rounded = prob.astype(BF16)
    dprob = jnp.concatenate([mm_t(x, y) for x, y in zip(g, v)], axis=0)
    dscore = prob * (dprob - jnp.sum(dprob * prob, axis=-1, keepdims=True))
    dscore = (dscore * SCALE).astype(BF16)
    pairs = range(HEADS // 2)
    dvs = [t_mm(rows_of(rounded, pair), g[pair]).astype(BF16) for pair in pairs]
    dqs = [join_heads(mm(rows_of(dscore, pair), k[pair])).astype(BF16) for pair in pairs]
    dks = [t_mm(rows_of(dscore, pair), q[pair]).astype(BF16) for pair in pairs]
    return jnp.concatenate(dqs + dks + dvs, axis=1)


def halves(ref, first):
    low = ref[:, 0, 0:PX, :].reshape(HALF, D)
    high = ref[:, 0, PX : 2 * PX, :].reshape(HALF, D)
    return jnp.where(first, low, high), jnp.where(first, high, low)


def regrouped(own_ref, other_ref, first):
    mine, theirs = halves(own_ref, first)[0], halves(other_ref, first)[0]
    return jnp.concatenate([jnp.where(first, mine, theirs), jnp.where(first, theirs, mine)], axis=0)


def k_first_stats(x_ref, stats_ref):
    low, high = x_ref[:, 0, 0:PX, :].reshape(HALF, D), x_ref[:, 0, PX : 2 * PX, :].reshape(HALF, D)
    tokens = jnp.concatenate([low, high], axis=0).astype(F32)
    spread_out(stats_ref, partial_stats(tokens, group_matrix()))


def normalized(x, rows, member):
    channels = to_channels(rows, member)
    return (x - per_token(channels[:VIEWS])) * per_token(channels[VIEWS:])


def k_view(entries, place, x_ref, other_ref, g_ref, wqkv_ref, wout_ref, stream_ref, saved_ref, sides_ref, own_ref, stats_ref):
    first = place[0] == 0
    member = group_matrix()
    sources = g_ref.shape[0]
    half = VIEWS // 2

    def side(low):
        chosen = range(low, low + sources // 2)
        means = [g_ref[s, a * half : (a + 1) * half, :] for s in chosen for a in range(2)]
        spreads = [g_ref[s, VIEWS + a * half : VIEWS + (a + 1) * half, :] for s in chosen for a in range(2)]
        return merge_stats(means, spreads, entries)

    low, high = side(0), side(sources // 2)
    rows = jnp.concatenate([low[0], high[0], low[1], high[1]], axis=0)
    own_ref[...] = rows
    x = regrouped(x_ref, other_ref, first).astype(F32)
    hidden = normalized(x, rows, member).astype(BF16)
    packed = mm(hidden, wqkv_ref[...]).astype(BF16)
    saved_ref[...] = packed
    mixed, _ = attend(packed, same_sequence(PX))
    sides_ref[:, :D] = hidden
    sides_ref[:, D:] = mixed
    stream = x + mm(mixed, wout_ref[...])
    stream_ref[...] = stream
    spread_out(stats_ref, partial_stats(stream, member))


def k_norm_two(entries, place, stream_ref, grad_ref, other_ref, g_ref, send_ref, rows_ref):
    member = group_matrix()
    sources = range(g_ref.shape[0])
    mean, inverse = merge_stats(
        [g_ref[s, 0:VIEWS, :] for s in sources], [g_ref[s, VIEWS:, :] for s in sources], entries
    )
    rows = jnp.concatenate([mean, inverse], axis=0)
    rows_ref[...] = rows
    shape = send_ref.shape[:2] + (D,)
    send_ref[:, :, :D] = normalized(stream_ref[...], rows, member).astype(BF16).reshape(shape)
    send_ref[:, :, D:] = regrouped(grad_ref, other_ref, place[0] == 0).reshape(shape)


def weight_sides(core, hidden, mixed, packed_grad, grad, keep_ref, give_ref):
    first = core == 0
    keep_ref[:, :D] = hidden
    give_ref[:, :D] = hidden
    keep_ref[:, D : 2 * D] = jnp.where(first, hidden, mixed)
    give_ref[:, D : 2 * D] = jnp.where(first, mixed, hidden)
    right_sides(core, packed_grad, grad, keep_ref, give_ref, 2 * D)


def right_sides(core, packed_grad, grad, keep_ref, give_ref, start=0):
    first = core == 0
    quarter = packed_grad[:, :D], packed_grad[:, D : 2 * D], packed_grad[:, 2 * D :], grad
    for slot in range(2):
        cols = slice(start + slot * D, start + (slot + 1) * D)
        keep_ref[:, cols] = jnp.where(first, quarter[slot], quarter[2 + slot])
        give_ref[:, cols] = jnp.where(first, quarter[2 + slot], quarter[slot])


def k_time(place, recv_ref, wqkv_ref, wout_ref, back_ref, keep_ref, give_ref):
    hidden = recv_ref[:, :, :D].reshape(T, D)
    grad = recv_ref[:, :, D:].reshape(T, D)
    allowed = same_sequence(recv_ref.shape[1])
    packed = mm(hidden, wqkv_ref[...]).astype(BF16)
    mixed, probs = attend(packed, allowed)
    shape = back_ref.shape[:2] + (D,)
    back_ref[:, :, :D] = mm(mixed, wout_ref[...]).astype(BF16).reshape(shape)
    packed_grad = attend_back(mm_t(grad, wout_ref[...]).astype(BF16), packed, allowed, probs)
    back_ref[:, :, D:] = mm_t(packed_grad, wqkv_ref[...]).astype(BF16).reshape(shape)
    weight_sides(place[1], hidden, mixed, packed_grad, grad, keep_ref, give_ref)


def k_back_stats(back_ref, stream_ref, rows_ref, stats_ref):
    member = group_matrix()
    grad = back_ref[:, :, D:].reshape(T, D).astype(F32)
    spread_out(stats_ref, both_sums(grad, normalized(stream_ref[...], rows_ref[...], member), member))


def k_view_back(entries, place, back_ref, stream_ref, rows_ref, g_ref, og_ref, ogother_ref, packed_ref, wout_ref,
                keep_ref, give_ref, pgrad_ref, stream_grad_ref, sums_ref):
    first = place[0] == 0
    member = group_matrix()
    sums = g_ref[0]
    for s in range(1, g_ref.shape[0]):
        sums = sums + g_ref[s]
    sums_ref[...] = sums
    channels = to_channels(jnp.concatenate([sums * (1.0 / entries), rows_ref[...]], axis=0), member)
    m1, m2, mean, inverse = (per_token(channels[k * VIEWS : (k + 1) * VIEWS]) for k in range(4))
    normed_two = (stream_ref[...] - mean) * inverse
    ghid = back_ref[:, :, D:].reshape(T, D).astype(F32)
    grad_stream = regrouped(og_ref, ogother_ref, first).astype(F32) + inverse * (ghid - m1 - normed_two * m2)
    stream_grad_ref[...] = grad_stream
    grad_b = grad_stream.astype(BF16)
    packed_grad = attend_back(mm_t(grad_b, wout_ref[...]).astype(BF16), packed_ref[...], same_sequence(PX))
    pgrad_ref[...] = packed_grad
    right_sides(place[1], packed_grad, grad_b, keep_ref, give_ref)


def k_view_stats(place, pgrad_ref, stream_grad_ref, back_ref, stream_ref, x_ref, other_ref, own_ref, wqkv_ref,
                 ukeep_ref, okeep_ref, send_ref, stats_ref):
    first = place[0] == 0
    member = group_matrix()
    grad = mm_t(pgrad_ref[...], wqkv_ref[...]).astype(BF16).astype(F32)
    channels = to_channels(own_ref[...], member)
    mean, inverse = per_token(channels[:VIEWS]), per_token(channels[VIEWS:])
    normed = (regrouped(x_ref, other_ref, first).astype(F32) - mean) * inverse
    stats_ref[...] = both_sums(grad, normed, member)
    partly = stream_grad_ref[...] + inverse * grad
    temporal = back_ref[:, :, :D].reshape(T, D).astype(F32)
    out = (stream_ref[...] + temporal).astype(BF16)
    ukeep_ref[...] = jnp.where(first, partly[:HALF], partly[HALF:])
    okeep_ref[...] = jnp.where(first, out[:HALF], out[HALF:])
    send_ref[:, :D] = jnp.where(first, partly[HALF:], partly[:HALF]).astype(BF16)
    send_ref[:, D:] = jnp.where(first, out[HALF:], out[:HALF])


def k_finish(entries, place, g_ref, sumstwo_ref, own_ref, x_ref, ukeep_ref, okeep_ref, recv_ref,
             out_ref, grad_ref, sums_ref):
    first = place[0] == 0
    member = group_matrix()
    half = VIEWS // 2
    sums = g_ref[...]

    def mine(rows):
        return jnp.where(first, rows[:half], rows[half:])

    s1, s2 = mine(sums[:VIEWS]), mine(sums[VIEWS:])
    sums_ref[0] = s1
    sums_ref[1] = s2
    sums_ref[2] = mine(sumstwo_ref[0:VIEWS, :])
    sums_ref[3] = mine(sumstwo_ref[VIEWS:, :])
    inverse = mine(own_ref[VIEWS:, :])
    scale = inverse * (1.0 / entries)
    rows = jnp.concatenate([mine(own_ref[0:VIEWS, :]), inverse, s1 * scale, s2 * scale], axis=0)
    channels = to_channels(rows, member)
    mean_c, inverse_c, a, b = (per_token(channels[k * half : (k + 1) * half]) for k in range(4))

    def finished(part, x):
        normed = (x.astype(F32) - mean_c) * inverse_c
        return (part.astype(F32) - a - normed * b).astype(BF16)

    x_keep, x_give = halves(x_ref, first)
    keep = finished(ukeep_ref[...], x_keep)
    other = finished(recv_ref[:, :D], x_give)
    shape = (half, PX, D)
    grad_ref[:, 0:PX, :] = jnp.where(first, keep, other).reshape(shape)
    grad_ref[:, PX:, :] = jnp.where(first, other, keep).reshape(shape)
    okeep, orecv = okeep_ref[...], recv_ref[:, D:]
    out_ref[:, 0:PX, :] = jnp.where(first, okeep, orecv).reshape(shape)
    out_ref[:, PX:, :] = jnp.where(first, orecv, okeep).reshape(shape)


def added32(*refs):
    total = refs[0][...].astype(F32)
    for ref in refs[1:]:
        total = total + ref[...].astype(F32)
    return total


def added(*refs):
    return added32(*refs).astype(BF16)


def split_rows(total, refs, cols=slice(None)):
    rows = total.shape[0] // len(refs)
    for s, ref in enumerate(refs):
        ref[:, cols] = total[s * rows : (s + 1) * rows].astype(BF16)


def weight_tile(unit, order, keep_ref, recv_ref):
    left = jnp.concatenate([keep_ref[:, unit * D : (unit + 1) * D], recv_ref[:, unit * D : (unit + 1) * D]], axis=0)
    cols = slice((2 + unit) * D, (3 + unit) * D)
    right = jnp.concatenate([keep_ref[:, cols], recv_ref[:, cols]], axis=0)
    return t_mm(mm(left, order).astype(BF16), right)


def k_weights_time(place, table_ref, keep_ref, recv_ref, *out_refs):
    order = (lax.broadcasted_iota(jnp.int32, (D, D), 0) == table_ref[place[2]]).astype(BF16)
    for unit in range(2):
        total = weight_tile(unit, order, keep_ref, recv_ref)
        split_rows(total, out_refs, slice(unit * D, (unit + 1) * D))


def k_left_sides(place, column_ref, mine_ref, theirs_ref, left_ref):
    first = place[1] == 0
    order = (lax.broadcasted_iota(jnp.int32, (D, D), 1) == column_ref[...]).astype(BF16)
    hidden = jnp.concatenate([mine_ref[:, :D], theirs_ref[:, :D]], axis=0)
    mixed = jnp.concatenate([mine_ref[:, D:], theirs_ref[:, D:]], axis=0)
    left_ref[0] = mm_t(order, hidden).astype(BF16)
    left_ref[1] = mm_t(order, jnp.where(first, hidden, mixed)).astype(BF16)


def k_weights_view(left_ref, mine_ref, theirs_ref, out_ref):
    for unit in range(2):
        cols = slice(unit * D, (unit + 1) * D)
        right = jnp.concatenate([mine_ref[:, cols], theirs_ref[:, cols]], axis=0)
        out_ref[:, cols] = mm(left_ref[unit], right).astype(BF16)


def k_sum_time(*refs):
    split_rows(added32(*refs[:4]), refs[4:])


def k_sum_rows(parts_ref, *refs):
    times, out_ref = refs[:4], refs[4]
    chips = out_ref.shape[0]
    rows = times[0].shape[0]
    count = parts_ref.shape[0] // rows
    parts = parts_ref[...].astype(F32)
    view = sum(parts[s * rows : (s + 1) * rows] for s in range(count))
    time = added32(*times)
    units = [view[:, :D], view[:, D:], time[:, :D], time[:, D:]]
    for row in range(out_ref.shape[2] // D):
        block = jnp.stack([unit[row * chips : (row + 1) * chips] for unit in units], axis=1)
        out_ref[:, :, row * D : (row + 1) * D] = block.astype(BF16)


def k_sum(parts_ref, out_ref):
    total = parts_ref[0].astype(F32)
    for s in range(1, parts_ref.shape[0]):
        total = total + parts_ref[s].astype(F32)
    out_ref[...] = total.astype(BF16)


def k_rows(place, own_ref, core_ref, view_ref, corner_ref, vqkv_ref, vout_ref, tqkv_ref, tout_ref):
    same, first = place[0] == place[1], place[1] == 0
    mine = jnp.where(same, own_ref[...].astype(F32), view_ref[...].astype(F32))
    other = jnp.where(same, core_ref[...].astype(F32), corner_ref[...].astype(F32))
    both = jnp.concatenate([jnp.where(first, mine, other), jnp.where(first, other, mine)], axis=0)
    rows = vout_ref.shape[0]

    def lines(unit):
        return jnp.concatenate([both[unit : unit + 1, row * D : (row + 1) * D] for row in range(rows)], axis=0)

    for unit, qkv_ref, out_ref in ((0, vqkv_ref, vout_ref), (2, tqkv_ref, tout_ref)):
        qkv_ref[...] = jnp.concatenate([lines(unit), lines(unit + 1), lines(unit + 4)], axis=1).astype(BF16)
        out_ref[...] = lines(unit + 5).astype(BF16)


def call(kernel, outs, *args, place=None, us=2, vmem=VMEM_LIMIT):
    specs = [pl.BlockSpec(memory_space=pltpu.VMEM)] * len(args)
    if place is not None:
        specs = [pl.BlockSpec(memory_space=pltpu.SMEM)] + specs
        args = (place,) + args
    return pl.pallas_call(
        kernel,
        out_shape=[jax.ShapeDtypeStruct(shape, dtype) for shape, dtype in outs],
        in_specs=specs,
        out_specs=[pl.BlockSpec(memory_space=pltpu.VMEM)] * len(outs),
        compiler_params=pltpu.CompilerParams(vmem_limit_bytes=vmem * 1024 * 1024),
        cost_estimate=pl.CostEstimate(flops=int(us * 1e9), bytes_accessed=int(us * 3e6), transcendentals=0),
    )(*args)


def row_tables(z, xl, core, dp):
    rows = D // (z * xl * core * dp)
    ring = core * xl
    chip = np.arange(z).reshape(1, 1, 1, z)
    row = np.arange(rows).reshape(1, 1, rows, 1)

    def place(y, x):
        return ((((chip * xl + x % xl) * core + x // xl) * dp + y) * rows + row).reshape(1, -1)

    table = []
    for me_x in range(ring):
        for me_dp in range(dp):
            y, x = (me_dp + np.arange(dp)) % dp, (me_x + np.arange(ring)) % ring
            table.append(place(y.reshape(dp, 1, 1, 1), x.reshape(1, ring, 1, 1)))
    absolute = place(np.arange(dp).reshape(1, dp, 1, 1), np.arange(ring).reshape(ring, 1, 1, 1))
    return np.stack(table).astype(np.int32), absolute.reshape(-1, 1).astype(np.int32)


def view_rows(*sizes):
    return row_tables(*sizes)[1]


def body(sizes, level_in, out_grad, view_qkv, view_out, time_qkv, time_out):
    z, xl, core, dp = sizes
    frames = z * xl * core
    entries = float(dp * 2 * PX * CH)
    frame_axes = ("z", "xl", "core")
    mates = ("view", "dp")
    group = 2 * dp
    spot = (lax.axis_index("view") * xl + lax.axis_index("xl")) * dp + lax.axis_index("dp")
    place = jnp.stack([lax.axis_index("view"), lax.axis_index("core"), spot]).astype(jnp.int32)
    table = jnp.asarray(row_tables(z, xl, core, dp)[0])
    rows = D // (z * xl * core * dp)
    stats = ((group, 2 * VIEWS, 128), F32)
    tok32, tok16 = ((T, D), F32), ((T, D), BF16)
    half32, half16 = ((HALF, D), F32), ((HALF, D), BF16)
    wide = ((T, 4 * D), BF16)
    moved = ((frames, T // frames, 2 * D), BF16)

    def share(field):
        return lax.all_to_all(field, mates, 0, 0, tiled=True)

    def transpose(field):
        return lax.all_to_all(field, frame_axes, 0, 0, tiled=True)

    def swap(field, axis):
        return lax.ppermute(field, axis, [(0, 1), (1, 0)])

    def shifted(pieces, axis):
        return [
            lax.ppermute(piece, axis, [(i, (i + step + 1) % 4) for i in range(4)]) for step, piece in enumerate(pieces)
        ]

    def crossed(field, step):
        return field + lax.ppermute(field, "dp", [(i, i ^ step) for i in range(dp)])

    views = VIEWS // 2
    rows16 = ((2 * VIEWS, 128), F32)
    x_other, og_other = swap(level_in, "view"), swap(out_grad, "view")
    (st1,) = call(k_first_stats, [stats], level_in)
    stream, packed_one, sides, own, st2 = call(
        functools.partial(k_view, entries), [tok32, ((T, 3 * D), BF16), ((T, 2 * D), BF16), rows16, stats],
        level_in, x_other, share(st1), view_qkv, view_out, place=place, us=4,
    )
    column = jnp.asarray(view_rows(z, xl, core, dp))
    (left,) = call(k_left_sides, [((2, D, 2 * T), BF16)], column, sides, swap(sides, "core"), place=place)
    out_field, rows_two = call(
        functools.partial(k_norm_two, entries), [moved, rows16], stream, out_grad, og_other, share(st2), place=place
    )
    back, keep_two, give_two = call(k_time, [moved, wide, wide], transpose(out_field), time_qkv, time_out, place=place, us=6)
    mine, *pieces = call(
        k_weights_time, [((D // 4, 2 * D), BF16)] * 4, table, keep_two, swap(give_two, "core"), place=place, us=3
    )
    moved_back, _, left = lax.optimization_barrier((transpose(back), pieces, left))
    time_parts = [mine, *shifted(pieces, "dp")]
    (st3,) = call(k_back_stats, [stats], moved_back, stream, rows_two, us=1)
    shared, time_parts = lax.optimization_barrier((share(st3), time_parts))
    keep_one, give_one, pgrad, stream_grad, sums_two = call(
        functools.partial(k_view_back, entries), [((T, 2 * D), BF16)] * 2 + [((T, 3 * D), BF16), tok32, rows16],
        moved_back, stream, rows_two, shared, out_grad, og_other, packed_one, view_out, place=place, us=5,
    )
    (partial,) = call(k_weights_view, [((D, 2 * D), BF16)], left, keep_one, swap(give_one, "core"), us=1)
    time_parts, partial, pgrad = lax.optimization_barrier((time_parts, partial, pgrad))
    u_keep, o_keep, send_back, st4 = call(
        k_view_stats, [half32, half16, ((HALF, 2 * D), BF16), rows16],
        pgrad, stream_grad, moved_back, stream, level_in, x_other, own, view_qkv, place=place, us=3,
    )
    parts = lax.all_to_all(partial, ("view", "xl", "dp"), 0, 0, tiled=True)
    mine, *pieces = call(k_sum_time, [((D // 16, 2 * D), BF16)] * 4, *time_parts)
    time_parts = [mine, *shifted(pieces, ("view", "xl"))]
    parts, time_parts, st4 = lax.optimization_barrier((parts, time_parts, crossed(crossed(st4, 2), 1)))
    (by_z,) = call(k_sum_rows, [((z, 4, rows * D), BF16)], parts, *time_parts)
    by_z, st4, send_back = lax.optimization_barrier((by_z, st4, send_back))
    by_z = lax.all_to_all(by_z, "z", 0, 0, tiled=True)
    recv_back = swap(send_back, "view")
    st4 = st4 + swap(st4, "view")
    by_z, st4, recv_back = lax.optimization_barrier((by_z, st4, recv_back))
    (summed,) = call(k_sum, [((4, rows * D), BF16)], by_z)
    level_out, level_in_grad, sums = call(
        functools.partial(k_finish, entries),
        [((views, 2 * PX, D), BF16), ((views, 2 * PX, D), BF16), ((4, views, 128), F32)],
        st4, sums_two, own, level_in, u_keep, o_keep, recv_back, place=place, us=3,
    )
    qkv_row, out_row = ((rows, 3 * D), BF16), ((rows, D), BF16)
    corner = lax.ppermute(summed, ("view", "core"), [(i, 3 - i) for i in range(4)])
    view_qkv_grad, view_out_grad, time_qkv_grad, time_out_grad = call(
        k_rows, [qkv_row, out_row, qkv_row, out_row],
        summed, swap(summed, "core"), swap(summed, "view"), corner, place=place,
    )
    return (
        level_out.reshape(level_in.shape),
        level_in_grad.reshape(level_in.shape),
        view_qkv_grad,
        view_out_grad,
        time_qkv_grad,
        time_out_grad,
        sums[:, :, :GROUPS].reshape(2, 2, views, 1, GROUPS),
    )


def solution(mesh):
    frames, dp = mesh.shape["frame"], mesh.shape["dp"]
    sizes = (frames // 4, 2, 2, dp)
    fine = Mesh(mesh.devices.reshape((2,) + sizes), ("view", "z", "xl", "core", "dp"))
    split = ("z", "xl", "core")
    tokens = P("view", split, "dp", None)
    rows = P(split + ("dp",), None)
    return jax.shard_map(
        functools.partial(body, sizes),
        mesh=fine,
        in_specs=(tokens, tokens, P(), P(), P(), P()),
        out_specs=(tokens, tokens, rows, rows, rows, rows, P(None, None, "view", split, None)),
        check_vma=False,
    )
```

```python
import functools

import jax
import jax.numpy as jnp
import numpy as np
from jax import lax
from jax.experimental import pallas as pl
from jax.experimental.pallas import tpu as pltpu
from jax.sharding import Mesh, PartitionSpec as P

HEADS = 10
HD = 64
GROUPS = 32
EPS = 1e-05
D = 640
CH = D // GROUPS
VIEWS = 8
PX = 16
T = VIEWS * PX
HALF = T // 2
SCALE = HD ** (-0.5)
F32 = jnp.float32
BF16 = jnp.bfloat16
VMEM_LIMIT = 32


def group_matrix():
    row = lax.broadcasted_iota(jnp.int32, (D, 128), 0)
    low = lax.broadcasted_iota(jnp.int32, (D, 128), 1) * CH
    return ((row >= low) & (row < low + CH)).astype(F32).astype(BF16)


def three_parts(rows):
    high = rows.astype(BF16)
    rest = rows - high.astype(F32)
    middle = rest.astype(BF16)
    return high, middle, (rest - middle.astype(F32)).astype(BF16)


def exact_product(rows, member, dims):
    count = rows.shape[0]
    stacked = jnp.concatenate([part.astype(F32) for part in three_parts(rows)], axis=0).astype(BF16)
    out = lax.dot_general(stacked, member, (dims, ((), ())), preferred_element_type=F32)
    return out[:count] + (out[count : 2 * count] + out[2 * count :])


def to_groups(rows, member):
    return exact_product(rows, member, ((1,), (0,)))


def to_channels(groups, member):
    return exact_product(groups, member, ((1,), (1,)))


def both_sums(grad, normed, member):
    return to_groups(jnp.concatenate([view_sum(grad), view_sum(grad * normed)], axis=0), member)


def view_sum(tokens):
    return jnp.sum(tokens.reshape(tokens.shape[0] // PX, PX, D), axis=1)


def per_token(rows):
    return jnp.broadcast_to(rows[:, None, :], (rows.shape[0], PX, D)).reshape(rows.shape[0] * PX, D)


def partial_stats(tokens, member):
    mean = to_groups(view_sum(tokens), member) * (1.0 / (PX * CH))
    centred = tokens - per_token(to_channels(mean, member))
    return jnp.concatenate([mean, to_groups(view_sum(centred * centred), member)], axis=0)


def merge_stats(means, spreads, entries):
    count = len(means)
    mean = sum(means) * (1.0 / count)
    spread = sum(spreads)
    for other in means:
        gap = other - mean
        spread = spread + gap * gap * float(PX * CH)
    return mean, lax.rsqrt(spread * (1.0 / entries) + EPS)


def spread_out(ref, both):
    ref[...] = jnp.broadcast_to(both[None], ref.shape)


def mm(left, right):
    return jnp.dot(left, right, preferred_element_type=F32)


def mm_t(left, right):
    return lax.dot_general(left, right, (((1,), (1,)), ((), ())), preferred_element_type=F32)


def t_mm(left, right):
    return lax.dot_general(left, right, (((0,), (0,)), ((), ())), preferred_element_type=F32)


def lane_low(rows):
    return lax.broadcasted_iota(jnp.int32, (rows, 128), 1) < HD


def both_heads(pair):
    low = lane_low(pair.shape[0])
    zero = jnp.zeros_like(pair)
    return jnp.concatenate([jnp.where(low, pair, zero), jnp.where(low, zero, pair)], axis=0)


def join_heads(stacked):
    return jnp.where(lane_low(T), stacked[:T], stacked[T:])


def same_sequence(period):
    row = lax.broadcasted_iota(jnp.int32, (2 * T, T), 0)
    col = lax.broadcasted_iota(jnp.int32, (2 * T, T), 1)
    return ((row ^ col) & (period - 1)) == 0


def softmax_all(stacked_q, keys, allowed):
    scores = jnp.concatenate([mm_t(q, k) for q, k in zip(stacked_q, keys)], axis=0)
    allowed = jnp.concatenate([allowed] * len(keys), axis=0)
    scores = jnp.where(allowed, scores * SCALE, -1e30)
    top = jnp.max(scores, axis=-1, keepdims=True)
    weights = jnp.exp(scores - top)
    return weights * (1.0 / jnp.sum(weights, axis=-1, keepdims=True))


def pair_of(index):
    return slice(index * 128, (index + 1) * 128)


def pieces_of(packed, first):
    return [packed[:, pair_of(first + pair)] for pair in range(HEADS // 2)]


def rows_of(stacked, pair):
    return stacked[pair * 2 * T : (pair + 1) * 2 * T]


def attend(packed, allowed):
    q, k, v = [both_heads(piece) for piece in pieces_of(packed, 0)], pieces_of(packed, 5), pieces_of(packed, 10)
    prob = softmax_all(q, k, allowed)
    rounded = prob.astype(BF16)
    outs = [join_heads(mm(rows_of(rounded, pair), v[pair])).astype(BF16) for pair in range(HEADS // 2)]
    return jnp.concatenate(outs, axis=1), prob


def attend_back(grad, packed, allowed, prob=None):
    q, k, v = [both_heads(piece) for piece in pieces_of(packed, 0)], pieces_of(packed, 5), pieces_of(packed, 10)
    g = [both_heads(piece) for piece in pieces_of(grad, 0)]
    if prob is None:
        prob = softmax_all(q, k, allowed)
    rounded = prob.astype(BF16)
    dprob = jnp.concatenate([mm_t(x, y) for x, y in zip(g, v)], axis=0)
    dscore = prob * (dprob - jnp.sum(dprob * prob, axis=-1, keepdims=True))
    dscore = (dscore * SCALE).astype(BF16)
    pairs = range(HEADS // 2)
    dvs = [t_mm(rows_of(rounded, pair), g[pair]).astype(BF16) for pair in pairs]
    dqs = [join_heads(mm(rows_of(dscore, pair), k[pair])).astype(BF16) for pair in pairs]
    dks = [t_mm(rows_of(dscore, pair), q[pair]).astype(BF16) for pair in pairs]
    return jnp.concatenate(dqs + dks + dvs, axis=1)


def halves(ref, first):
    low = ref[:, 0, 0:PX, :].reshape(HALF, D)
    high = ref[:, 0, PX : 2 * PX, :].reshape(HALF, D)
    return jnp.where(first, low, high), jnp.where(first, high, low)


def regrouped(own_ref, other_ref, first):
    mine, theirs = halves(own_ref, first)[0], halves(other_ref, first)[0]
    return jnp.concatenate([jnp.where(first, mine, theirs), jnp.where(first, theirs, mine)], axis=0)


def k_first_stats(place, x_ref, stats_ref):
    low, high = x_ref[:, 0, 0:PX, :].reshape(HALF, D), x_ref[:, 0, PX : 2 * PX, :].reshape(HALF, D)
    tokens = jnp.concatenate([low, high], axis=0).astype(F32)
    spread_out(stats_ref, partial_stats(tokens, group_matrix()))


def normalized(x, rows, member):
    channels = to_channels(rows, member)
    return (x - per_token(channels[:VIEWS])) * per_token(channels[VIEWS:])


def k_view(entries, place, x_ref, other_ref, g_ref, wqkv_ref, wout_ref, stream_ref, saved_ref, sides_ref, own_ref, stats_ref):
    first = place[0] == 0
    member = group_matrix()
    sources = g_ref.shape[0]
    half = VIEWS // 2

    def side(low):
        chosen = range(low, low + sources // 2)
        means = [g_ref[s, a * half : (a + 1) * half, :] for s in chosen for a in range(2)]
        spreads = [g_ref[s, VIEWS + a * half : VIEWS + (a + 1) * half, :] for s in chosen for a in range(2)]
        return merge_stats(means, spreads, entries)

    low, high = side(0), side(sources // 2)
    rows = jnp.concatenate([low[0], high[0], low[1], high[1]], axis=0)
    own_ref[...] = rows
    x = regrouped(x_ref, other_ref, first).astype(F32)
    hidden = normalized(x, rows, member).astype(BF16)
    packed = mm(hidden, wqkv_ref[...]).astype(BF16)
    saved_ref[...] = packed
    mixed, _ = attend(packed, same_sequence(PX))
    sides_ref[:, :D] = hidden
    sides_ref[:, D:] = mixed
    stream = x + mm(mixed, wout_ref[...])
    stream_ref[...] = stream
    spread_out(stats_ref, partial_stats(stream, member))


def k_norm_two(entries, place, stream_ref, grad_ref, other_ref, g_ref, send_ref, rows_ref):
    member = group_matrix()
    sources = range(g_ref.shape[0])
    mean, inverse = merge_stats(
        [g_ref[s, 0:VIEWS, :] for s in sources], [g_ref[s, VIEWS:, :] for s in sources], entries
    )
    rows = jnp.concatenate([mean, inverse], axis=0)
    rows_ref[...] = rows
    shape = send_ref.shape[:2] + (D,)
    send_ref[:, :, :D] = normalized(stream_ref[...], rows, member).astype(BF16).reshape(shape)
    send_ref[:, :, D:] = regrouped(grad_ref, other_ref, place[0] == 0).reshape(shape)


def weight_sides(core, hidden, mixed, packed_grad, grad, keep_ref, give_ref):
    first = core == 0
    keep_ref[:, :D] = hidden
    give_ref[:, :D] = hidden
    keep_ref[:, D : 2 * D] = jnp.where(first, hidden, mixed)
    give_ref[:, D : 2 * D] = jnp.where(first, mixed, hidden)
    right_sides(core, packed_grad, grad, keep_ref, give_ref, 2 * D)


def right_sides(core, packed_grad, grad, keep_ref, give_ref, start=0):
    first = core == 0
    quarter = packed_grad[:, :D], packed_grad[:, D : 2 * D], packed_grad[:, 2 * D :], grad
    for slot in range(2):
        cols = slice(start + slot * D, start + (slot + 1) * D)
        keep_ref[:, cols] = jnp.where(first, quarter[slot], quarter[2 + slot])
        give_ref[:, cols] = jnp.where(first, quarter[2 + slot], quarter[slot])


def k_time(place, recv_ref, wqkv_ref, wout_ref, back_ref, keep_ref, give_ref):
    hidden = recv_ref[:, :, :D].reshape(T, D)
    grad = recv_ref[:, :, D:].reshape(T, D)
    allowed = same_sequence(recv_ref.shape[1])
    packed = mm(hidden, wqkv_ref[...]).astype(BF16)
    mixed, probs = attend(packed, allowed)
    shape = back_ref.shape[:2] + (D,)
    back_ref[:, :, :D] = mm(mixed, wout_ref[...]).astype(BF16).reshape(shape)
    packed_grad = attend_back(mm_t(grad, wout_ref[...]).astype(BF16), packed, allowed, probs)
    back_ref[:, :, D:] = mm_t(packed_grad, wqkv_ref[...]).astype(BF16).reshape(shape)
    weight_sides(place[1], hidden, mixed, packed_grad, grad, keep_ref, give_ref)


def k_back_stats(back_ref, stream_ref, rows_ref, stats_ref):
    member = group_matrix()
    grad = back_ref[:, :, D:].reshape(T, D).astype(F32)
    spread_out(stats_ref, both_sums(grad, normalized(stream_ref[...], rows_ref[...], member), member))


def k_view_back(entries, place, back_ref, stream_ref, rows_ref, g_ref, og_ref, ogother_ref, packed_ref, wout_ref,
                keep_ref, give_ref, pgrad_ref, stream_grad_ref, sums_ref):
    first = place[0] == 0
    member = group_matrix()
    sums = g_ref[0]
    for s in range(1, g_ref.shape[0]):
        sums = sums + g_ref[s]
    sums_ref[...] = sums
    channels = to_channels(jnp.concatenate([sums * (1.0 / entries), rows_ref[...]], axis=0), member)
    m1, m2, mean, inverse = (per_token(channels[k * VIEWS : (k + 1) * VIEWS]) for k in range(4))
    normed_two = (stream_ref[...] - mean) * inverse
    ghid = back_ref[:, :, D:].reshape(T, D).astype(F32)
    grad_stream = regrouped(og_ref, ogother_ref, first).astype(F32) + inverse * (ghid - m1 - normed_two * m2)
    stream_grad_ref[...] = grad_stream
    grad_b = grad_stream.astype(BF16)
    packed_grad = attend_back(mm_t(grad_b, wout_ref[...]).astype(BF16), packed_ref[...], same_sequence(PX))
    pgrad_ref[...] = packed_grad
    right_sides(place[1], packed_grad, grad_b, keep_ref, give_ref)


def k_view_stats(place, pgrad_ref, stream_grad_ref, back_ref, stream_ref, x_ref, other_ref, own_ref, wqkv_ref,
                 ukeep_ref, okeep_ref, send_ref, stats_ref):
    first = place[0] == 0
    member = group_matrix()
    grad = mm_t(pgrad_ref[...], wqkv_ref[...]).astype(BF16).astype(F32)
    channels = to_channels(own_ref[...], member)
    mean, inverse = per_token(channels[:VIEWS]), per_token(channels[VIEWS:])
    normed = (regrouped(x_ref, other_ref, first).astype(F32) - mean) * inverse
    stats_ref[...] = both_sums(grad, normed, member)
    partly = stream_grad_ref[...] + inverse * grad
    temporal = back_ref[:, :, :D].reshape(T, D).astype(F32)
    out = (stream_ref[...] + temporal).astype(BF16)
    ukeep_ref[...] = jnp.where(first, partly[:HALF], partly[HALF:])
    okeep_ref[...] = jnp.where(first, out[:HALF], out[HALF:])
    send_ref[:, :D] = jnp.where(first, partly[HALF:], partly[:HALF]).astype(BF16)
    send_ref[:, D:] = jnp.where(first, out[HALF:], out[:HALF])


def k_finish(entries, place, g_ref, sumstwo_ref, own_ref, x_ref, ukeep_ref, okeep_ref, recv_ref,
             out_ref, grad_ref, sums_ref):
    first = place[0] == 0
    member = group_matrix()
    half = VIEWS // 2
    sums = g_ref[...]

    def mine(rows):
        return jnp.where(first, rows[:half], rows[half:])

    s1, s2 = mine(sums[:VIEWS]), mine(sums[VIEWS:])
    sums_ref[0] = s1
    sums_ref[1] = s2
    sums_ref[2] = mine(sumstwo_ref[0:VIEWS, :])
    sums_ref[3] = mine(sumstwo_ref[VIEWS:, :])
    inverse = mine(own_ref[VIEWS:, :])
    scale = inverse * (1.0 / entries)
    rows = jnp.concatenate([mine(own_ref[0:VIEWS, :]), inverse, s1 * scale, s2 * scale], axis=0)
    channels = to_channels(rows, member)
    mean_c, inverse_c, a, b = (per_token(channels[k * half : (k + 1) * half]) for k in range(4))

    def finished(part, x):
        normed = (x.astype(F32) - mean_c) * inverse_c
        return (part.astype(F32) - a - normed * b).astype(BF16)

    x_keep, x_give = halves(x_ref, first)
    keep = finished(ukeep_ref[...], x_keep)
    other = finished(recv_ref[:, :D], x_give)
    shape = (half, PX, D)
    grad_ref[:, 0:PX, :] = jnp.where(first, keep, other).reshape(shape)
    grad_ref[:, PX:, :] = jnp.where(first, other, keep).reshape(shape)
    okeep, orecv = okeep_ref[...], recv_ref[:, D:]
    out_ref[:, 0:PX, :] = jnp.where(first, okeep, orecv).reshape(shape)
    out_ref[:, PX:, :] = jnp.where(first, orecv, okeep).reshape(shape)


def added32(*refs):
    total = refs[0][...].astype(F32)
    for ref in refs[1:]:
        total = total + ref[...].astype(F32)
    return total


def added(*refs):
    return added32(*refs).astype(BF16)


def split_rows(total, refs, cols=slice(None)):
    rows = total.shape[0] // len(refs)
    for s, ref in enumerate(refs):
        ref[:, cols] = total[s * rows : (s + 1) * rows].astype(BF16)


def weight_tile(unit, order, keep_ref, recv_ref):
    left = jnp.concatenate([keep_ref[:, unit * D : (unit + 1) * D], recv_ref[:, unit * D : (unit + 1) * D]], axis=0)
    cols = slice((2 + unit) * D, (3 + unit) * D)
    right = jnp.concatenate([keep_ref[:, cols], recv_ref[:, cols]], axis=0)
    return t_mm(mm(left, order).astype(BF16), right)


def k_weights_time(place, table_ref, keep_ref, recv_ref, *out_refs):
    order = (lax.broadcasted_iota(jnp.int32, (D, D), 0) == table_ref[place[2]]).astype(BF16)
    for unit in range(2):
        total = weight_tile(unit, order, keep_ref, recv_ref)
        split_rows(total, out_refs, slice(unit * D, (unit + 1) * D))


def k_left_sides(place, column_ref, mine_ref, theirs_ref, left_ref):
    first = place[1] == 0
    order = (lax.broadcasted_iota(jnp.int32, (D, D), 1) == column_ref[...]).astype(BF16)
    hidden = jnp.concatenate([mine_ref[:, :D], theirs_ref[:, :D]], axis=0)
    mixed = jnp.concatenate([mine_ref[:, D:], theirs_ref[:, D:]], axis=0)
    left_ref[0] = mm_t(order, hidden).astype(BF16)
    left_ref[1] = mm_t(order, jnp.where(first, hidden, mixed)).astype(BF16)


def k_weights_view(left_ref, mine_ref, theirs_ref, out_ref):
    for unit in range(2):
        cols = slice(unit * D, (unit + 1) * D)
        right = jnp.concatenate([mine_ref[:, cols], theirs_ref[:, cols]], axis=0)
        out_ref[:, cols] = mm(left_ref[unit], right).astype(BF16)


def k_sum_time(*refs):
    split_rows(added32(*refs[:4]), refs[4:])


def k_sum_rows(parts_ref, *refs):
    times, out_ref = refs[:4], refs[4]
    chips = out_ref.shape[0]
    rows = times[0].shape[0]
    count = parts_ref.shape[0] // rows
    parts = parts_ref[...].astype(F32)
    view = sum(parts[s * rows : (s + 1) * rows] for s in range(count))
    time = added32(*times)
    units = [view[:, :D], view[:, D:], time[:, :D], time[:, D:]]
    for row in range(out_ref.shape[2] // D):
        block = jnp.stack([unit[row * chips : (row + 1) * chips] for unit in units], axis=1)
        out_ref[:, :, row * D : (row + 1) * D] = block.astype(BF16)


def k_sum(parts_ref, out_ref):
    total = parts_ref[0].astype(F32)
    for s in range(1, parts_ref.shape[0]):
        total = total + parts_ref[s].astype(F32)
    out_ref[...] = total.astype(BF16)


def k_rows(place, own_ref, core_ref, view_ref, corner_ref, vqkv_ref, vout_ref, tqkv_ref, tout_ref):
    same, first = place[0] == place[1], place[1] == 0
    mine = jnp.where(same, own_ref[...].astype(F32), view_ref[...].astype(F32))
    other = jnp.where(same, core_ref[...].astype(F32), corner_ref[...].astype(F32))
    both = jnp.concatenate([jnp.where(first, mine, other), jnp.where(first, other, mine)], axis=0)
    rows = vout_ref.shape[0]

    def lines(unit):
        return jnp.concatenate([both[unit : unit + 1, row * D : (row + 1) * D] for row in range(rows)], axis=0)

    for unit, qkv_ref, out_ref in ((0, vqkv_ref, vout_ref), (2, tqkv_ref, tout_ref)):
        qkv_ref[...] = jnp.concatenate([lines(unit), lines(unit + 1), lines(unit + 4)], axis=1).astype(BF16)
        out_ref[...] = lines(unit + 5).astype(BF16)


def call(kernel, outs, *args, place=None, us=2, vmem=VMEM_LIMIT):
    specs = [pl.BlockSpec(memory_space=pltpu.VMEM)] * len(args)
    if place is not None:
        specs = [pl.BlockSpec(memory_space=pltpu.SMEM)] + specs
        args = (place,) + args
    return pl.pallas_call(
        kernel,
        out_shape=[jax.ShapeDtypeStruct(shape, dtype) for shape, dtype in outs],
        in_specs=specs,
        out_specs=[pl.BlockSpec(memory_space=pltpu.VMEM)] * len(outs),
        compiler_params=pltpu.CompilerParams(vmem_limit_bytes=vmem * 1024 * 1024),
        cost_estimate=pl.CostEstimate(flops=int(us * 1e9), bytes_accessed=int(us * 3e6), transcendentals=0),
    )(*args)


def row_tables(z, xl, core, dp):
    rows = D // (z * xl * core * dp)
    ring = core * xl
    chip = np.arange(z).reshape(1, 1, 1, z)
    row = np.arange(rows).reshape(1, 1, rows, 1)

    def place(y, x):
        return ((((chip * xl + x % xl) * core + x // xl) * dp + y) * rows + row).reshape(1, -1)

    table = []
    for me_x in range(ring):
        for me_dp in range(dp):
            y, x = (me_dp + np.arange(dp)) % dp, (me_x + np.arange(ring)) % ring
            table.append(place(y.reshape(dp, 1, 1, 1), x.reshape(1, ring, 1, 1)))
    absolute = place(np.arange(dp).reshape(1, dp, 1, 1), np.arange(ring).reshape(ring, 1, 1, 1))
    return np.stack(table).astype(np.int32), absolute.reshape(-1, 1).astype(np.int32)


def view_rows(*sizes):
    return row_tables(*sizes)[1]


def body(sizes, level_in, out_grad, view_qkv, view_out, time_qkv, time_out):
    z, xl, core, dp = sizes
    frames = z * xl * core
    entries = float(dp * 2 * PX * CH)
    frame_axes = ("z", "xl", "core")
    mates = ("view", "dp")
    group = 2 * dp
    spot = (lax.axis_index("view") * xl + lax.axis_index("xl")) * dp + lax.axis_index("dp")
    place = jnp.stack([lax.axis_index("view"), lax.axis_index("core"), spot]).astype(jnp.int32)
    table = jnp.asarray(row_tables(z, xl, core, dp)[0])
    rows = D // (z * xl * core * dp)
    stats = ((group, 2 * VIEWS, 128), F32)
    tok32, tok16 = ((T, D), F32), ((T, D), BF16)
    half32, half16 = ((HALF, D), F32), ((HALF, D), BF16)
    wide = ((T, 4 * D), BF16)
    moved = ((frames, T // frames, 2 * D), BF16)

    def share(field):
        return lax.all_to_all(field, mates, 0, 0, tiled=True)

    def transpose(field):
        return lax.all_to_all(field, frame_axes, 0, 0, tiled=True)

    def swap(field, axis):
        return lax.ppermute(field, axis, [(0, 1), (1, 0)])

    def shifted(pieces, axis):
        return [
            lax.ppermute(piece, axis, [(i, (i + step + 1) % 4) for i in range(4)]) for step, piece in enumerate(pieces)
        ]

    def crossed(field, step):
        return field + lax.ppermute(field, "dp", [(i, i ^ step) for i in range(dp)])

    views = VIEWS // 2
    rows16 = ((2 * VIEWS, 128), F32)
    x_other = swap(level_in, "view")
    (st1,) = call(k_first_stats, [stats], level_in, place=place)
    stream, packed_one, sides, own, st2 = call(
        functools.partial(k_view, entries), [tok32, ((T, 3 * D), BF16), ((T, 2 * D), BF16), rows16, stats],
        level_in, x_other, share(st1), view_qkv, view_out, place=place, us=4,
    )
    column = jnp.asarray(view_rows(z, xl, core, dp))
    (left,) = call(k_left_sides, [((2, D, 2 * T), BF16)], column, sides, swap(sides, "core"), place=place)
    late_grad, st2 = lax.optimization_barrier((out_grad, st2))
    og_other = swap(late_grad, "view")
    out_field, rows_two = call(
        functools.partial(k_norm_two, entries), [moved, rows16], stream, out_grad, og_other, share(st2), place=place
    )
    back, keep_two, give_two = call(k_time, [moved, wide, wide], transpose(out_field), time_qkv, time_out, place=place, us=6)
    mine, *pieces = call(
        k_weights_time, [((D // 4, 2 * D), BF16)] * 4, table, keep_two, swap(give_two, "core"), place=place, us=3
    )
    moved_back, _, left = lax.optimization_barrier((transpose(back), pieces, left))
    time_parts = [mine, *shifted(pieces, "dp")]
    (st3,) = call(k_back_stats, [stats], moved_back, stream, rows_two, us=1)
    shared, time_parts = lax.optimization_barrier((share(st3), time_parts))
    keep_one, give_one, pgrad, stream_grad, sums_two = call(
        functools.partial(k_view_back, entries), [((T, 2 * D), BF16)] * 2 + [((T, 3 * D), BF16), tok32, rows16],
        moved_back, stream, rows_two, shared, out_grad, og_other, packed_one, view_out, place=place, us=5,
    )
    (partial,) = call(k_weights_view, [((D, 2 * D), BF16)], left, keep_one, swap(give_one, "core"), us=1)
    time_parts, partial, pgrad = lax.optimization_barrier((time_parts, partial, pgrad))
    u_keep, o_keep, send_back, st4 = call(
        k_view_stats, [half32, half16, ((HALF, 2 * D), BF16), rows16],
        pgrad, stream_grad, moved_back, stream, level_in, x_other, own, view_qkv, place=place, us=3,
    )
    parts = lax.all_to_all(partial, ("view", "xl", "dp"), 0, 0, tiled=True)
    mine, *pieces = call(k_sum_time, [((D // 16, 2 * D), BF16)] * 4, *time_parts)
    time_parts = [mine, *shifted(pieces, ("view", "xl"))]
    parts, time_parts, st4 = lax.optimization_barrier((parts, time_parts, crossed(crossed(st4, 2), 1)))
    (by_z,) = call(k_sum_rows, [((z, 4, rows * D), BF16)], parts, *time_parts)
    by_z, st4, send_back = lax.optimization_barrier((by_z, st4, send_back))
    by_z = lax.all_to_all(by_z, "z", 0, 0, tiled=True)
    recv_back = swap(send_back, "view")
    st4 = st4 + swap(st4, "view")
    by_z, st4, recv_back = lax.optimization_barrier((by_z, st4, recv_back))
    (summed,) = call(k_sum, [((4, rows * D), BF16)], by_z)
    level_out, level_in_grad, sums = call(
        functools.partial(k_finish, entries),
        [((views, 2 * PX, D), BF16), ((views, 2 * PX, D), BF16), ((4, views, 128), F32)],
        st4, sums_two, own, level_in, u_keep, o_keep, recv_back, place=place, us=3,
    )
    qkv_row, out_row = ((rows, 3 * D), BF16), ((rows, D), BF16)
    corner = lax.ppermute(summed, ("view", "core"), [(i, 3 - i) for i in range(4)])
    view_qkv_grad, view_out_grad, time_qkv_grad, time_out_grad = call(
        k_rows, [qkv_row, out_row, qkv_row, out_row],
        summed, swap(summed, "core"), swap(summed, "view"), corner, place=place,
    )
    return (
        level_out.reshape(level_in.shape),
        level_in_grad.reshape(level_in.shape),
        view_qkv_grad,
        view_out_grad,
        time_qkv_grad,
        time_out_grad,
        sums[:, :, :GROUPS].reshape(2, 2, views, 1, GROUPS),
    )


def solution(mesh):
    frames, dp = mesh.shape["frame"], mesh.shape["dp"]
    sizes = (frames // 4, 2, 2, dp)
    fine = Mesh(mesh.devices.reshape((2,) + sizes), ("view", "z", "xl", "core", "dp"))
    split = ("z", "xl", "core")
    tokens = P("view", split, "dp", None)
    rows = P(split + ("dp",), None)
    return jax.shard_map(
        functools.partial(body, sizes),
        mesh=fine,
        in_specs=(tokens, tokens, P(), P(), P(), P()),
        out_specs=(tokens, tokens, rows, rows, rows, rows, P(None, None, "view", split, None)),
        check_vma=False,
    )
```
